32 devices in a mesh: space: 8 (over z, y), tm: 4 (over x, core).
Axes of the slice: x: 2, y: 2, z: 4, core: 2. Of those that a mesh axis runs over, the one named last changes fastest.
Arguments:
- snapshots: bfloat16 [8192, 16384], P('space', 'tm'), may hold values from -1200 to 1200
- pod_basis: bfloat16 [8192, 96], P('space'), may hold values from -0.0625 to 0.0625
- inputs: bfloat16 [112, 16384], P(None, 'tm'), may hold values from -20 to 20
Outputs:
- factored: float32 [4864, 4864], P('tm', 'space')
The draws below stay inside these ranges and needn't reach their ends.
All inputs are finite; a program needn't handle non-finite values.
Results may differ from the reference program's by a relative error of at most 0.0031.
Values may be sent and summed in bfloat16 or wider, within the bound.
No kernel may reach another device: no remote copies, remote signals or barrier semaphores. Data moves between devices by JAX's collectives and lax.ppermute only.
A program may use at most 192 MiB of HBM per device.

```python
import jax
import jax.numpy as jnp
import numpy as np
from jax import lax

R = 96
U = 112
NB = 128
P_SIZE = 4864
NDOF = 8192
NSNAP = 16384


def draw_snapshots(key, part):
    key_base, key_rows, key_cols = jax.random.split(key, 3)
    row_scale = 10.0 ** jax.random.uniform(key_rows, (NDOF, 1), jnp.float32)
    ramp = 3.0 ** (jnp.arange(NSNAP, dtype=jnp.float32) / (NSNAP - 1))
    col_scale = 10.0 ** jax.random.uniform(key_cols, (1, NSNAP), jnp.float32) * ramp[None, :]
    base = jnp.clip(jax.random.normal(key_base, (NDOF, NSNAP), jnp.float32), -4.0, 4.0)
    return (base * row_scale * col_scale).astype(jnp.bfloat16)


def draw_inputs(key, part):
    key_base, key_cols = jax.random.split(key, 2)
    col_scale = 0.5 * 10.0 ** jax.random.uniform(key_cols, (1, NSNAP), jnp.float32)
    base = jnp.clip(jax.random.normal(key_base, (U, NSNAP), jnp.float32), -4.0, 4.0)
    return (base * col_scale).astype(jnp.bfloat16)


def shard_levels(key, dims, shards, smallest, top_value):
    factor_of, own = 1.0, jax.random.fold_in(key, 6)
    for dim, blocks in shards:
        steps = jnp.exp(jax.random.uniform(jax.random.fold_in(own, dim), (blocks,), jnp.float32, smallest / len(shards), top_value / len(shards)))
        factor_of = factor_of * jnp.repeat(steps, dims[dim] // blocks).reshape([-1 if axis == dim else 1 for axis in range(len(dims))])
    return factor_of


def normal_values(stream_key, extent, scale, limit, shards=(), kind=jnp.bfloat16):
    values = scale * jax.random.normal(stream_key, extent, jnp.float32)
    if shards:
        values = values * shard_levels(stream_key, extent, shards, -0.22, 0.18)
    return jnp.clip(values, -limit, limit).astype(kind)


def setup_inputs(seed: int = 0) -> dict:
    key_of = jax.random.split(jax.random.key(seed), 4)
    snapshots = draw_snapshots(jax.random.fold_in(key_of[3], 71), 0)
    pod_basis = normal_values(key_of[1], (NDOF, R), NDOF ** -0.5, 0.0625, ((0, 8),))
    inputs = draw_inputs(jax.random.fold_in(key_of[3], 71), 0)
    return {"snapshots": snapshots, "pod_basis": pod_basis, "inputs": inputs}


EPS = 1e-06
REG = 0.5

def feature_tables(mode_count, input_count):
    upper_i, upper_j = np.triu_indices(mode_count)
    first_index = np.concatenate([np.arange(mode_count), upper_i, mode_count + 1 + np.arange(input_count)]).astype(np.int32)
    second_index = np.concatenate([np.full(mode_count, mode_count), upper_j, np.full(input_count, mode_count)]).astype(np.int32)
    return (first_index, second_index)

def reference(snapshots, pod_basis, inputs):
    coords = jnp.dot(pod_basis.T.astype(jnp.float32), snapshots.astype(jnp.float32), preferred_element_type=jnp.float32)
    energy = lax.optimization_barrier(jnp.sum(coords * coords, axis=1)) / NSNAP
    scaled = coords / jnp.sqrt(energy + EPS)[:, None]
    extended = jnp.concatenate([scaled, jnp.ones((1, NSNAP), jnp.float32), inputs.astype(jnp.float32)], axis=0)
    first_index, second_index = feature_tables(R, U)
    features = (extended[jnp.asarray(first_index)] * extended[jnp.asarray(second_index)]).astype(jnp.bfloat16)
    gram = jnp.dot(features.astype(jnp.float32), features.T.astype(jnp.float32), preferred_element_type=jnp.float32) / NSNAP + REG * jnp.eye(P_SIZE, dtype=jnp.float32)
    panel_full = gram[:, :NB]
    corner = jnp.linalg.cholesky(panel_full[:NB])
    panel_factor = jax.scipy.linalg.solve_triangular(corner, panel_full.T, lower=True).T
    trailing = gram - jnp.dot(panel_factor, panel_factor.T, precision=lax.Precision.HIGHEST)
    row_ids = jnp.arange(P_SIZE, dtype=jnp.int32)[:, None]
    col_ids = jnp.arange(P_SIZE, dtype=jnp.int32)[None, :]
    left_part = jnp.pad(panel_factor, ((0, 0), (0, P_SIZE - NB)))
    return jnp.where(col_ids < NB, left_part, jnp.where(row_ids < NB, jnp.zeros_like(trailing), trailing))
```

```python
import functools
import math

import jax
import jax.numpy as jnp
import numpy as np
from jax import lax
from jax.experimental import pallas as pl
from jax.experimental.pallas import tpu as pltpu
from jax.sharding import PartitionSpec as P

NB = 128
EPS = 1e-06
REG = 0.5
PAD = 8
LANES = 128


def feature_pairs(modes, count):
    first, second = np.triu_indices(modes)
    lead = [(f, None) for f in range(modes)]
    pairs = list(zip(first.tolist(), second.tolist()))
    tail = [(modes + k, None) for k in range(count)]
    return lead + pairs + tail


def runs_of(rows):
    runs = []
    for at, row in enumerate(rows):
        if row is None:
            continue
        a, b = row
        key = ("one", a - at) if b is None else (a, b - at)
        if runs and runs[-1][2] == key and runs[-1][1] == at:
            runs[-1][1] = at + 1
        else:
            runs.append([at, at + 1, key])
    return runs


def build_rows(x_ref, f_ref, lane, rows, base, extra=None):
    sub = lax.broadcasted_iota(jnp.int32, (8, LANES), 0)
    cache = {}

    def row_of(a):
        if a not in cache:
            cache.clear()
            cache[a] = jnp.broadcast_to(x_ref[lane, PAD + a : PAD + a + 1, :], (8, LANES))
        return cache[a]

    def eight(at):
        chunk = rows[at : at + 8]
        chunk = chunk + [None] * (8 - len(chunk))
        total = None
        for lo, hi, (a, shift) in runs_of(chunk):
            part = x_ref[lane, PAD + shift : PAD + shift + 8, :]
            if a != "one":
                part = part * row_of(a)
            if total is None and lo == 0:
                total = part
            else:
                if total is None:
                    total = jnp.zeros((8, LANES), jnp.float32)
                total = jnp.where(sub >= lo, part, total)
            last = hi
        if total is None:
            return jnp.zeros((8, LANES), jnp.float32)
        if last < 8:
            total = jnp.where(sub < last, total, 0.0)
        return total

    for at in range(0, len(rows), 16):
        value = jnp.concatenate([eight(at), eight(at + 8)], axis=0).astype(jnp.bfloat16)
        f_ref[base + at : base + at + 16, pl.ds(pl.multiple_of(lane * LANES, LANES), LANES)] = value


def gram_kernel(plan, where_ref, x_in, u_in, inv_ref, acc_in, acc_ref, x_ref, f_ref):
    step = pl.program_id(0)
    modes, row_sets, col_sets, head_set, row_count, a_rows, b_rows = plan
    depth = x_in.shape[-1]
    lanes = depth // LANES

    @pl.when(step == 0)
    def _():
        f_ref[...] = jnp.zeros_like(f_ref)
        x_ref[...] = jnp.zeros_like(x_ref)
        if acc_in is None:
            acc_ref[...] = jnp.zeros_like(acc_ref)
        else:
            acc_ref[...] = acc_in[...]

    scale = inv_ref[...]
    for lane in range(lanes):
        at = slice(lane * LANES, (lane + 1) * LANES)
        x_ref[lane, PAD : PAD + modes, :] = x_in[0, :, at].astype(jnp.float32) * scale
        x_ref[lane, PAD + modes : PAD + modes + u_in.shape[1], :] = u_in[0, :, at].astype(jnp.float32)

    for number, rows in enumerate(row_sets):
        @pl.when(where_ref[0] == number)
        def _(rows=rows):
            @pl.loop(0, lanes)
            def _(lane):
                build_rows(x_ref, f_ref, lane, rows, 0)

    @pl.loop(0, lanes)
    def _(lane):
        build_rows(x_ref, f_ref, lane, head_set, row_count)

    for number, rows in enumerate(col_sets):
        @pl.when(where_ref[1] == number)
        def _(rows=rows):
            @pl.loop(0, lanes)
            def _(lane):
                build_rows(x_ref, f_ref, lane, rows, row_count + NB)

    left = f_ref[0:a_rows, :]
    for at in range(0, b_rows, 256):
        wide = min(256, b_rows - at)
        right = f_ref[row_count + at : row_count + at + wide, :]
        acc_ref[:, at : at + wide] += lax.dot_general(
            left, right, (((1,), (1,)), ((), ())), preferred_element_type=jnp.float32
        )


def make_plan(modes, count, time_count, space_count):
    pairs = feature_pairs(modes, count)
    total = len(pairs)
    row_count, col_count = total // time_count, total // space_count
    row_sets = [pairs[t * row_count : (t + 1) * row_count] for t in range(time_count)]
    col_sets = [pairs[s * col_count : (s + 1) * col_count] for s in range(space_count)]
    a_rows = row_count + NB
    b_rows = -(-(NB + col_count) // 128) * 128
    return modes, row_sets, col_sets, pairs[:NB], row_count, a_rows, b_rows


def gram_call(plan, where, x, u, inv, acc=None):
    modes, _, col_sets, _, row_count, a_rows, b_rows = plan
    steps, _, depth = x.shape
    groups = u.shape[0]
    per = steps // groups
    inputs = u.shape[1]
    lanes = depth // LANES
    in_specs = [
        pl.BlockSpec((1, modes, depth), lambda k, w: (k, 0, 0)),
        pl.BlockSpec((1, inputs, depth), lambda k, w: (k // per, 0, w[2 + k % per])),
        pl.BlockSpec((modes, 1), lambda k, w: (0, 0)),
    ]
    args = [x, u, inv]
    body = functools.partial(gram_kernel, plan)
    if acc is None:
        inner = lambda w, a, b, c, o, s1, s2: body(w, a, b, c, None, o, s1, s2)
    else:
        inner = body
        in_specs.append(pl.BlockSpec((a_rows, b_rows), lambda k, w: (0, 0)))
        args.append(acc)
    return pl.pallas_call(
        inner,
        grid_spec=pltpu.PrefetchScalarGridSpec(
            num_scalar_prefetch=1,
            grid=(steps,),
            in_specs=in_specs,
            out_specs=pl.BlockSpec((a_rows, b_rows), lambda k, w: (0, 0)),
            scratch_shapes=[
                pltpu.VMEM((lanes, PAD + modes + inputs + 8, LANES), jnp.float32),
                pltpu.VMEM((-(-(row_count + b_rows) // 16) * 16, depth), jnp.bfloat16),
            ],
        ),
        out_shape=jax.ShapeDtypeStruct((a_rows, b_rows), jnp.float32),
        compiler_params=pltpu.CompilerParams(vmem_limit_bytes=56 * 1024 * 1024, dimension_semantics=("arbitrary",)),
        name="gram",
    )(where, *args)


def inverse_factor(corner):
    sub = lax.broadcasted_iota(jnp.int32, (8, 2 * NB), 0)
    row_ids = lax.broadcasted_iota(jnp.int32, (NB, NB), 0)
    col_ids = lax.broadcasted_iota(jnp.int32, (NB, NB), 1)
    eye = (row_ids == col_ids).astype(jnp.float32)
    joined = jnp.concatenate([corner, eye], axis=1)
    tiles = [joined[at : at + 8] for at in range(0, NB, 8)]
    for k in range(NB):
        q, r = divmod(k, 8)
        row = tiles[q][r : r + 1]
        row = row * (1.0 / row[:, k : k + 1])
        for p in range(q, NB // 8):
            column = tiles[p][:, k : k + 1]
            change = column * row
            if p == q:
                change = jnp.where(sub > r, change, 0.0)
            tiles[p] = tiles[p] - change
    done = jnp.concatenate(tiles, axis=0)
    pivots = jnp.sum(done[:, :NB] * eye, axis=1, keepdims=True)
    return done[:, NB:] * lax.rsqrt(pivots)


def dot32(a, b, dims):
    return lax.dot_general(
        a, b, (dims, ((), ())), precision=lax.Precision.HIGHEST, preferred_element_type=jnp.float32
    )


def finish_kernel(snaps, row_count, col_count, where_ref, acc_ref, out_ref):
    t, s = where_ref[0], where_ref[1]
    head = pl.ds(row_count, NB)
    row_ids = lax.broadcasted_iota(jnp.int32, (NB, NB), 0)
    col_ids = lax.broadcasted_iota(jnp.int32, (NB, NB), 1)
    eye = REG * (row_ids == col_ids).astype(jnp.float32)
    corner = acc_ref[head, 0:NB] * (1.0 / snaps) + eye
    inverse = inverse_factor(corner)
    cols = acc_ref[head, NB : NB + col_count] * (1.0 / snaps)
    all_rows = lax.broadcasted_iota(jnp.int32, (NB, col_count), 0)
    all_cols = s * col_count + lax.broadcasted_iota(jnp.int32, (NB, col_count), 1)
    cols = cols + REG * (all_rows == all_cols).astype(jnp.float32)
    cols_factor = dot32(inverse, cols, ((1,), (0,)))
    for at in range(0, row_count, NB):
        tall = min(NB, row_count - at)
        rows = slice(at, at + tall)
        ids = t * row_count + at + lax.broadcasted_iota(jnp.int32, (tall, col_count), 0)
        cids = s * col_count + lax.broadcasted_iota(jnp.int32, (tall, col_count), 1)
        side = acc_ref[rows, 0:NB] * (1.0 / snaps)
        side = side + REG * (ids[:, :NB] == lax.broadcasted_iota(jnp.int32, (tall, NB), 1)).astype(jnp.float32)
        factor = dot32(side, inverse, ((1,), (1,)))
        gram = acc_ref[rows, NB : NB + col_count] * (1.0 / snaps)
        gram = gram + REG * (ids == cids).astype(jnp.float32)
        value = gram - dot32(factor, cols_factor, ((1,), (0,)))
        value = jnp.where(ids < NB, 0.0, value)
        out_ref[rows, NB:col_count] = value[:, NB:]
        out_ref[rows, 0:NB] = jnp.where(s == 0, factor, value[:, :NB])


def finish(where, acc, snaps, row_count, col_count):
    return pl.pallas_call(
        functools.partial(finish_kernel, snaps, row_count, col_count),
        in_specs=[pl.BlockSpec(memory_space=pltpu.SMEM), pl.BlockSpec(memory_space=pltpu.VMEM)],
        out_specs=pl.BlockSpec(memory_space=pltpu.VMEM),
        out_shape=jax.ShapeDtypeStruct((row_count, col_count), jnp.float32),
        compiler_params=pltpu.CompilerParams(vmem_limit_bytes=40 * 1024 * 1024),
        name="finish",
    )(where, acc)


def swap(x, axis, bit):
    return lax.ppermute(x, axis, [(i, i ^ bit) for i in range(lax.axis_size(axis))])


def shards(snapshots, pod_basis, inputs):
    modes = pod_basis.shape[1]
    space_count, time_count = lax.axis_size("space"), lax.axis_size("tm")
    t, s = lax.axis_index("tm"), lax.axis_index("space")
    local = snapshots.shape[1]
    snaps = local * time_count
    depth = local // space_count
    plan = make_plan(modes, inputs.shape[0], time_count, space_count)
    row_count = plan[4]
    col_count = len(plan[2][0])
    last = space_count - 1

    pairs = [(a * time_count + b, a * time_count + (b ^ 2)) for a in range(space_count) for b in range(time_count) if a == last or b < 2]
    u_far = lax.ppermute(inputs, ("space", "tm"), pairs)
    pairs = [(a * time_count + b, a * time_count + (b ^ 1)) for a in range(space_count) for b in range(time_count) if a == last or b == 2]
    u_pair = lax.ppermute(jnp.stack([inputs, u_far]), ("space", "tm"), pairs)
    u_near = jnp.stack([inputs, u_pair[0]])
    u_far = jnp.stack([u_far, u_pair[1]])

    limit = 1200.0 * 0.0625 * snapshots.shape[0] * space_count
    shrink = 2.0 ** -max(0, math.ceil(math.log2(limit / 65000.0)))
    part = jnp.einsum("dr,ds->rs", pod_basis, snapshots, preferred_element_type=jnp.float32)
    part = (part * shrink).astype(jnp.float16)
    part = part.reshape(modes, space_count, depth).transpose(1, 0, 2)
    part = lax.all_to_all(part, "space", 0, 0, tiled=False)
    mine = jnp.sum(part.astype(jnp.float32), axis=0).astype(jnp.float16)[None]
    order = [0]
    bit = space_count // 2
    while bit:
        mine = jnp.concatenate([mine, swap(mine, "space", bit)], axis=0)
        order = order + [o ^ bit for o in order]
        bit //= 2
    own = mine.astype(jnp.float32)
    energy = lax.psum(jnp.sum(own * own, axis=(0, 2)), "tm") / (snaps * shrink * shrink)
    inv = (shrink ** -1 / jnp.sqrt(energy + EPS))[:, None]
    where = jnp.concatenate([jnp.stack([t, s]), s ^ jnp.asarray(order, jnp.int32)]).astype(jnp.int32)
    far = swap(mine, "tm", 2)
    x_near = jnp.concatenate([own, swap(mine, "tm", 1).astype(jnp.float32)], axis=0)
    acc = gram_call(plan, where, x_near, u_near, inv)
    x_far = jnp.concatenate([far, swap(far, "tm", 1)], axis=0).astype(jnp.float32)
    acc = gram_call(plan, where, x_far, u_far, inv, acc)
    return finish(where, acc, snaps, row_count, col_count)


def solution(mesh):
    return jax.shard_map(
        shards,
        mesh=mesh,
        in_specs=(P("space", "tm"), P("space", None), P(None, "tm")),
        out_specs=P("tm", "space"),
        check_vma=False,
    )
```

```python
import functools
import math

import jax
import jax.numpy as jnp
import numpy as np
from jax import lax
from jax.experimental import pallas as pl
from jax.experimental.pallas import tpu as pltpu
from jax.sharding import PartitionSpec as P

NB = 128
EPS = 1e-06
REG = 0.5
PAD = 8
LANES = 128


def feature_pairs(modes, count):
    first, second = np.triu_indices(modes)
    lead = [(f, None) for f in range(modes)]
    pairs = list(zip(first.tolist(), second.tolist()))
    tail = [(modes + k, None) for k in range(count)]
    return lead + pairs + tail


def runs_of(rows):
    runs = []
    for at, row in enumerate(rows):
        if row is None:
            continue
        a, b = row
        key = ("one", a - at) if b is None else (a, b - at)
        if runs and runs[-1][2] == key and runs[-1][1] == at:
            runs[-1][1] = at + 1
        else:
            runs.append([at, at + 1, key])
    return runs


def build_rows(x_ref, f_ref, lane, rows, base):
    sub = lax.broadcasted_iota(jnp.int32, (8, LANES), 0)
    cache = {}

    def row_of(a):
        if a not in cache:
            cache.clear()
            cache[a] = jnp.broadcast_to(x_ref[lane, PAD + a : PAD + a + 1, :], (8, LANES))
        return cache[a]

    def eight(at):
        chunk = rows[at : at + 8]
        chunk = chunk + [None] * (8 - len(chunk))
        total = None
        for lo, hi, (a, shift) in runs_of(chunk):
            part = x_ref[lane, PAD + shift : PAD + shift + 8, :]
            if a != "one":
                part = part * row_of(a)
            if total is None and lo == 0:
                total = part
            else:
                if total is None:
                    total = jnp.zeros((8, LANES), jnp.float32)
                total = jnp.where(sub >= lo, part, total)
            last = hi
        if total is None:
            return jnp.zeros((8, LANES), jnp.float32)
        if last < 8:
            total = jnp.where(sub < last, total, 0.0)
        return total

    for at in range(0, len(rows), 16):
        value = jnp.concatenate([eight(at), eight(at + 8)], axis=0).astype(jnp.bfloat16)
        f_ref[base + at : base + at + 16, pl.ds(pl.multiple_of(lane * LANES, LANES), LANES)] = value


def gram_kernel(plan, snaps, closing, where_ref, own_ref, near_ref, u_own, u_near, inv_ref, *refs):
    modes, row_sets, col_sets, head_set, row_count, a_rows, b_rows = plan
    if closing:
        acc_in, out_ref, acc_ref, prior_ref, sem, x_ref, f_ref = refs
    else:
        acc_ref, x_ref, f_ref = refs
    step, steps = pl.program_id(0), pl.num_programs(0)
    slots, _, slot_depth = own_ref.shape
    per = slot_depth // LANES
    lanes = slots * per
    inputs = u_own.shape[0]

    @pl.when(step == 0)
    def _():
        if closing:
            pltpu.make_async_copy(acc_in, prior_ref, sem).start()
        f_ref[...] = jnp.zeros_like(f_ref)
        x_ref[...] = jnp.zeros_like(x_ref)
        acc_ref[...] = jnp.zeros_like(acc_ref)

    scale = inv_ref[...]

    def prepare(x_in, u_in, first_slot):
        for slot in range(slots):
            source = where_ref[2 + first_slot + slot] * slot_depth
            for lane in range(per):
                at = slice(lane * LANES, (lane + 1) * LANES)
                x_ref[slot * per + lane, PAD : PAD + modes, :] = x_in[slot, :, at] * scale
                u_at = pl.ds(pl.multiple_of(source + lane * LANES, LANES), LANES)
                x_ref[slot * per + lane, PAD + modes : PAD + modes + inputs, :] = u_in[:, u_at].astype(jnp.float32)

    half = steps // 2
    pl.when(step < half)(lambda: prepare(own_ref, u_own, step * slots))
    pl.when(step >= half)(lambda: prepare(near_ref, u_near, (step - half) * slots))

    def build(rows, base):
        @pl.loop(0, lanes)
        def _(lane):
            build_rows(x_ref, f_ref, lane, rows, base)

    for number, rows in enumerate(row_sets):
        pl.when(where_ref[0] == number)(lambda rows=rows: build(rows, 0))
    build(head_set, row_count)
    for number, rows in enumerate(col_sets):
        pl.when(where_ref[1] == number)(lambda rows=rows: build(rows, a_rows))

    left = f_ref[0:a_rows, :]
    for at in range(0, b_rows, 256):
        wide = min(256, b_rows - at)
        right = f_ref[row_count + at : row_count + at + wide, :]
        acc_ref[:, at : at + wide] += lax.dot_general(
            left, right, (((1,), (1,)), ((), ())), preferred_element_type=jnp.float32
        )

    if closing:
        @pl.when(step == steps - 1)
        def _():
            pltpu.make_async_copy(acc_in, prior_ref, sem).wait()
            finish(snaps, row_count, len(col_sets[0]), where_ref, acc_ref, prior_ref, out_ref)


def make_plan(modes, count, time_count, space_count):
    pairs = feature_pairs(modes, count)
    total = len(pairs)
    row_count, col_count = total // time_count, total // space_count
    row_sets = [pairs[t * row_count : (t + 1) * row_count] for t in range(time_count)]
    col_sets = [pairs[s * col_count : (s + 1) * col_count] for s in range(space_count)]
    a_rows = row_count + NB
    b_rows = -(-(NB + col_count) // 128) * 128
    return modes, row_sets, col_sets, pairs[:NB], row_count, a_rows, b_rows


def gram_call(plan, snaps, where, own, near, u_own, u_near, inv, acc=None, depth=2048):
    modes, _, col_sets, _, row_count, a_rows, b_rows = plan
    total, _, slot_depth = own.shape
    inputs = u_own.shape[0]
    slots = depth // slot_depth
    half = total // slots
    lanes = depth // LANES
    closing = acc is not None
    whole = lambda shape: pl.BlockSpec(shape, lambda k, w: (0,) * len(shape))
    block = (slots, modes, slot_depth)
    in_specs = [
        pl.BlockSpec(block, lambda k, w: (jnp.minimum(k, half - 1), 0, 0)),
        pl.BlockSpec(block, lambda k, w: (jnp.maximum(k - half, 0), 0, 0)),
        whole(u_own.shape),
        whole(u_near.shape),
        whole((modes, 1)),
    ]
    args = [own, near, u_own, u_near, inv]
    acc_shape = (a_rows, b_rows)
    scratch = [
        pltpu.VMEM((lanes, PAD + modes + inputs + 8, LANES), jnp.float32),
        pltpu.VMEM((-(-(row_count + b_rows) // 16) * 16, depth), jnp.bfloat16),
    ]
    out_shape = acc_shape
    if closing:
        in_specs.append(pl.BlockSpec(memory_space=pl.ANY))
        args.append(acc)
        scratch = [pltpu.VMEM(acc_shape, jnp.float32)] * 2 + [pltpu.SemaphoreType.DMA] + scratch
        out_shape = (row_count, len(col_sets[0]))
    flops = 2 * a_rows * b_rows * 2 * total * slot_depth
    return pl.pallas_call(
        functools.partial(gram_kernel, plan, snaps, closing),
        grid_spec=pltpu.PrefetchScalarGridSpec(
            num_scalar_prefetch=1,
            grid=(2 * half,),
            in_specs=in_specs,
            out_specs=whole(out_shape),
            scratch_shapes=scratch,
        ),
        out_shape=jax.ShapeDtypeStruct(out_shape, jnp.float32),
        compiler_params=pltpu.CompilerParams(
            vmem_limit_bytes=56 * 1024 * 1024, dimension_semantics=("arbitrary",)
        ),
        cost_estimate=pl.CostEstimate(flops=2 * flops, bytes_accessed=20_000_000, transcendentals=0),
        name="close" if closing else "gram",
    )(where, *args)


def inverse_factor(corner):
    sub = lax.broadcasted_iota(jnp.int32, (8, 2 * NB), 0)
    row_ids = lax.broadcasted_iota(jnp.int32, (NB, NB), 0)
    col_ids = lax.broadcasted_iota(jnp.int32, (NB, NB), 1)
    eye = (row_ids == col_ids).astype(jnp.float32)
    joined = jnp.concatenate([corner, eye], axis=1)
    tiles = [joined[at : at + 8] for at in range(0, NB, 8)]
    for k in range(NB):
        q, r = divmod(k, 8)
        row = tiles[q][r : r + 1]
        row = row * (1.0 / row[:, k : k + 1])
        for p in range(q, NB // 8):
            column = tiles[p][:, k : k + 1]
            change = column * row
            if p == q:
                change = jnp.where(sub > r, change, 0.0)
            tiles[p] = tiles[p] - change
    done = jnp.concatenate(tiles, axis=0)
    pivots = jnp.sum(done[:, :NB] * eye, axis=1, keepdims=True)
    return done[:, NB:] * lax.rsqrt(pivots)


def dot32(a, b, dims):
    return lax.dot_general(
        a, b, (dims, ((), ())), precision=lax.Precision.HIGHEST, preferred_element_type=jnp.float32
    )


def finish(snaps, row_count, col_count, where_ref, acc_ref, prior_ref, out_ref):
    t, s = where_ref[0], where_ref[1]
    head = slice(row_count, row_count + NB)

    def gram_part(rows, cols, row_start, col_start):
        value = (acc_ref[rows, cols] + prior_ref[rows, cols]) * (1.0 / snaps)
        row_ids = row_start + lax.broadcasted_iota(jnp.int32, value.shape, 0)
        col_ids = col_start + lax.broadcasted_iota(jnp.int32, value.shape, 1)
        return value + REG * (row_ids == col_ids).astype(jnp.float32), row_ids

    own = slice(NB, NB + col_count)
    inverse = inverse_factor(gram_part(head, slice(0, NB), 0, 0)[0])
    cols_factor = dot32(inverse, gram_part(head, own, 0, s * col_count)[0], ((1,), (0,)))
    for at in range(0, row_count, NB):
        rows = slice(at, min(at + NB, row_count))
        factor = dot32(gram_part(rows, slice(0, NB), t * row_count + at, 0)[0], inverse, ((1,), (1,)))
        value, row_ids = gram_part(rows, own, t * row_count + at, s * col_count)
        value = value - dot32(factor, cols_factor, ((1,), (0,)))
        value = jnp.where(row_ids < NB, 0.0, value)
        out_ref[rows, NB:col_count] = value[:, NB:]
        out_ref[rows, 0:NB] = jnp.where(s == 0, factor, value[:, :NB])


def swap(x, axis, bit):
    return lax.ppermute(x, axis, [(i, i ^ bit) for i in range(lax.axis_size(axis))])


def shards(snapshots, pod_basis, inputs):
    modes = pod_basis.shape[1]
    space_count, time_count = lax.axis_size("space"), lax.axis_size("tm")
    t, s = lax.axis_index("tm"), lax.axis_index("space")
    local = snapshots.shape[1]
    snaps = local * time_count
    depth = local // space_count
    plan = make_plan(modes, inputs.shape[0], time_count, space_count)

    def some(x, bit, wanted):
        pairs = [
            (a * time_count + b, a * time_count + (b ^ bit))
            for a in range(space_count)
            for b in range(time_count)
            if a == space_count - 1 or b in wanted
        ]
        return lax.ppermute(x, ("space", "tm"), pairs)

    u_near = some(inputs, 1, (2,))
    u_far = some(inputs, 2, (0, 1))
    u_far_near = some(u_far, 1, (2,))

    limit = 1200.0 * 0.0625 * snapshots.shape[0] * space_count
    shrink = 2.0 ** -max(0, math.ceil(math.log2(limit / 65000.0)))
    part = jnp.einsum("dr,ds->rs", pod_basis, snapshots, preferred_element_type=jnp.float32)
    part = (part * shrink).astype(jnp.float16)
    part = part.reshape(modes, space_count, depth).transpose(1, 0, 2)
    part = lax.all_to_all(part, "space", 0, 0, tiled=False)
    mine = jnp.sum(part.astype(jnp.float32), axis=0).astype(jnp.float16)[None]
    order = [0]
    bit = space_count // 2
    while bit:
        if bit == 1:
            wide = mine.astype(jnp.float32)
            energy = jnp.sum(wide * wide, axis=(0, 2))
            for axis, step in (("space", 1), ("tm", 1), ("tm", 2)):
                energy = energy + swap(energy, axis, step)
        mine = jnp.concatenate([mine, swap(mine, "space", bit)], axis=0)
        order = order + [o ^ bit for o in order]
        bit //= 2
    mine, energy = lax.optimization_barrier((mine, energy))
    inv = (shrink ** -1 / jnp.sqrt(energy / (snaps * shrink * shrink) + EPS))[:, None]
    where = jnp.concatenate([jnp.stack([t, s]), s ^ jnp.asarray(order, jnp.int32)]).astype(jnp.int32)
    far = swap(mine, "tm", 2)
    near = swap(mine, "tm", 1)
    acc = gram_call(plan, snaps, where, mine.astype(jnp.float32), near.astype(jnp.float32), inputs, u_near, inv)
    far_near = swap(far, "tm", 1)
    return gram_call(
        plan, snaps, where, far.astype(jnp.float32), far_near.astype(jnp.float32), u_far, u_far_near, inv, acc
    )


def solution(mesh):
    return jax.shard_map(
        shards,
        mesh=mesh,
        in_specs=(P("space", "tm"), P("space", None), P(None, "tm")),
        out_specs=P("tm", "space"),
        check_vma=False,
    )
```

```python
import functools
import math

import jax
import jax.numpy as jnp
import numpy as np
from jax import lax
from jax.experimental import pallas as pl
from jax.experimental.pallas import tpu as pltpu
from jax.sharding import PartitionSpec as P

NB = 128
EPS = 1e-06
REG = 0.5
PAD = 8
LANES = 128


def feature_pairs(modes, count):
    first, second = np.triu_indices(modes)
    lead = [(f, None) for f in range(modes)]
    pairs = list(zip(first.tolist(), second.tolist()))
    tail = [(modes + k, None) for k in range(count)]
    return lead + pairs + tail


def runs_of(rows):
    runs = []
    for at, row in enumerate(rows):
        if row is None:
            continue
        a, b = row
        key = ("one", a - at) if b is None else (a, b - at)
        if runs and runs[-1][2] == key and runs[-1][1] == at:
            runs[-1][1] = at + 1
        else:
            runs.append([at, at + 1, key])
    return runs


def build_rows(x_ref, f_ref, lane, rows, base):
    sub = lax.broadcasted_iota(jnp.int32, (8, LANES), 0)
    cache = {}

    def row_of(a):
        if a not in cache:
            cache.clear()
            cache[a] = jnp.broadcast_to(x_ref[lane, PAD + a : PAD + a + 1, :], (8, LANES))
        return cache[a]

    def eight(at):
        chunk = rows[at : at + 8]
        chunk = chunk + [None] * (8 - len(chunk))
        total = None
        for lo, hi, (a, shift) in runs_of(chunk):
            part = x_ref[lane, PAD + shift : PAD + shift + 8, :]
            if a != "one":
                part = part * row_of(a)
            if total is None and lo == 0:
                total = part
            else:
                if total is None:
                    total = jnp.zeros((8, LANES), jnp.float32)
                total = jnp.where(sub >= lo, part, total)
            last = hi
        if total is None:
            return jnp.zeros((8, LANES), jnp.float32)
        if last < 8:
            total = jnp.where(sub < last, total, 0.0)
        return total

    for at in range(0, len(rows), 16):
        value = jnp.concatenate([eight(at), eight(at + 8)], axis=0).astype(jnp.bfloat16)
        f_ref[base + at : base + at + 16, pl.ds(pl.multiple_of(lane * LANES, LANES), LANES)] = value


def gram_kernel(plan, snaps, closing, feed, where_ref, *refs):
    modes, row_sets, col_sets, head_set, row_count, a_rows, b_rows = plan
    pieces, sources, tables = feed
    x_ins, refs = refs[: sum(pieces)], refs[sum(pieces) :]
    u_ins, refs = refs[: max(sources) + 1], refs[max(sources) + 1 :]
    inv_ref, refs = refs[0], refs[1:]
    if closing:
        acc_in, out_ref, acc_ref, acc_sem = refs[:4]
        prior = pltpu.make_async_copy(acc_in, acc_ref, acc_sem)
    else:
        acc_ref = refs[0]
    x_buf, x_sem, u_buf, u_sem, x_ref, f_ref = refs[-6:]
    step, steps = pl.program_id(0), len(pieces)
    _, slots, inputs, slot_depth = u_buf.shape
    per = slot_depth // LANES
    lanes = slots * per
    wanted = jnp.logical_or(where_ref[0] == len(row_sets) - 1, where_ref[1] == len(col_sets) - 1)

    def x_copies(number):
        copies, at = [], 0
        for piece in range(pieces[number]):
            ref = x_ins[sum(pieces[:number]) + piece]
            copies.append(
                pltpu.make_async_copy(ref, x_buf.at[number % 2, at : at + ref.shape[0]], x_sem.at[number % 2, piece])
            )
            at += ref.shape[0]
        return copies

    def u_copies(number):
        for slot in range(slots):
            chunk = where_ref[2 + tables[number] * slots + slot]
            at = pl.ds(pl.multiple_of(chunk * slot_depth, slot_depth), slot_depth)
            yield pltpu.make_async_copy(
                u_ins[sources[number]].at[:, at], u_buf.at[number % 2, slot], u_sem.at[number % 2, slot]
            )

    def fetch(number):
        for copy in x_copies(number):
            copy.start()
        pl.when(wanted)(lambda: [copy.start() for copy in u_copies(number)] and None)

    def arrive(number):
        for copy in x_copies(number):
            copy.wait()
        pl.when(wanted)(lambda: [copy.wait() for copy in u_copies(number)] and None)

    @pl.when(step == 0)
    def _():
        fetch(0)
        if closing:
            prior.start()
        else:
            acc_ref[...] = jnp.zeros_like(acc_ref)

    scale = inv_ref[...]
    for number in range(steps):
        @pl.when(step == number)
        def _(number=number):
            if number + 1 < steps:
                fetch(number + 1)
            arrive(number)
            now = number % 2
            for lane in range(lanes):
                at = slice(lane % per * LANES, (lane % per + 1) * LANES)
                x_ref[lane, PAD : PAD + modes, :] = x_buf[now, lane // per, :, at] * scale

            @pl.when(wanted)
            def _():
                for lane in range(lanes):
                    at = slice(lane % per * LANES, (lane % per + 1) * LANES)
                    rows = slice(PAD + modes, PAD + modes + inputs)
                    x_ref[lane, rows, :] = u_buf[now, lane // per, :, at].astype(jnp.float32)

    def build(rows, base):
        @pl.loop(0, lanes)
        def _(lane):
            build_rows(x_ref, f_ref, lane, rows, base)

    for number, rows in enumerate(row_sets):
        pl.when(where_ref[0] == number)(lambda rows=rows: build(rows, 0))
    build(head_set, row_count)
    for number, rows in enumerate(col_sets):
        pl.when(where_ref[1] == number)(lambda rows=rows: build(rows, a_rows))

    if closing:
        pl.when(step == 0)(prior.wait)
    left = f_ref[0:a_rows, :]
    for at in range(0, b_rows, 256):
        wide = min(256, b_rows - at)
        right = f_ref[row_count + at : row_count + at + wide, :]
        acc_ref[:, at : at + wide] += lax.dot_general(
            left, right, (((1,), (1,)), ((), ())), preferred_element_type=jnp.float32
        )

    if closing:
        @pl.when(step == steps - 1)
        def _():
            finish(snaps, row_count, len(col_sets[0]), where_ref, acc_ref, out_ref)


def make_plan(modes, count, time_count, space_count):
    pairs = feature_pairs(modes, count)
    total = len(pairs)
    row_count, col_count = total // time_count, total // space_count
    row_sets = [pairs[t * row_count : (t + 1) * row_count] for t in range(time_count)]
    col_sets = [pairs[s * col_count : (s + 1) * col_count] for s in range(space_count)]
    a_rows = row_count + NB
    b_rows = -(-(NB + col_count) // 128) * 128
    return modes, row_sets, col_sets, pairs[:NB], row_count, a_rows, b_rows


def gram_call(plan, snaps, where, xs, us, sources, tables, inv, acc=None):
    modes, _, col_sets, _, row_count, a_rows, b_rows = plan
    inputs = us[0].shape[0]
    slot_depth = xs[0][0].shape[2]
    slots = sum(piece.shape[0] for piece in xs[0])
    depth = slots * slot_depth
    lanes = depth // LANES
    steps = len(xs)
    pieces = [len(x) for x in xs]
    closing = acc is not None
    args = [piece for x in xs for piece in x] + list(us)
    in_specs = [pl.BlockSpec(memory_space=pl.ANY)] * len(args)
    args.append(inv)
    in_specs.append(pl.BlockSpec((modes, 1), lambda k, w: (0, 0)))
    acc_shape = out_shape = (a_rows, b_rows)
    scratch = [
        pltpu.VMEM((2, slots, modes, slot_depth), jnp.float32),
        pltpu.SemaphoreType.DMA((2, max(pieces))),
        pltpu.VMEM((2, slots, inputs, slot_depth), jnp.bfloat16),
        pltpu.SemaphoreType.DMA((2, slots)),
        pltpu.VMEM((lanes, PAD + modes + inputs + 8, LANES), jnp.float32),
        pltpu.VMEM((-(-(row_count + b_rows) // 16) * 16, depth), jnp.bfloat16),
    ]
    if closing:
        in_specs.append(pl.BlockSpec(memory_space=pl.ANY))
        args.append(acc)
        scratch = [pltpu.VMEM(acc_shape, jnp.float32), pltpu.SemaphoreType.DMA] + scratch
        out_shape = (row_count, len(col_sets[0]))
    flops = 2 * a_rows * b_rows * steps * depth
    return pl.pallas_call(
        functools.partial(gram_kernel, plan, snaps, closing, (pieces, sources, tables)),
        grid_spec=pltpu.PrefetchScalarGridSpec(
            num_scalar_prefetch=1,
            grid=(steps,),
            in_specs=in_specs,
            out_specs=pl.BlockSpec(out_shape, lambda k, w: (0, 0)),
            scratch_shapes=scratch,
        ),
        out_shape=jax.ShapeDtypeStruct(out_shape, jnp.float32),
        compiler_params=pltpu.CompilerParams(
            vmem_limit_bytes=56 * 1024 * 1024, dimension_semantics=("arbitrary",)
        ),
        cost_estimate=pl.CostEstimate(flops=2 * flops, bytes_accessed=20_000_000, transcendentals=0),
        name="close" if closing else "gram",
    )(where, *args)


def inverse_factor(corner):
    row_ids = lax.broadcasted_iota(jnp.int32, (NB, NB), 0)
    col_ids = lax.broadcasted_iota(jnp.int32, (NB, NB), 1)
    eye = (row_ids == col_ids).astype(jnp.float32)
    sub = lax.broadcasted_iota(jnp.int32, (8, NB), 0)
    left = [corner[at : at + 8] for at in range(0, NB, 8)]
    right = [eye[at : at + 8] for at in range(0, NB, 8)]
    spread = lambda x: jnp.broadcast_to(x, (8, NB))
    out = []
    for q in range(NB // 8):
        columns = [spread(left[q][:, 8 * q + c : 8 * q + c + 1]) for c in range(8)]
        a = {(r, c): spread(columns[c][r : r + 1, :]) for r in range(8) for c in range(r + 1)}
        low = {}
        invd = []
        for k in range(8):
            inv = 1.0 / a[k, k]
            invd.append(inv)
            for r in range(k + 1, 8):
                low[r, k] = a[r, k] * inv
            for r in range(k + 1, 8):
                for c in range(k + 1, r + 1):
                    a[r, c] = a[r, c] - low[r, k] * a[c, k]
            w = {}
        for c in range(8):
            for r in range(c + 1, 8):
                v = low[r, c]
                for m in range(c + 1, r):
                    v = v + low[r, m] * w[m, c]
                w[r, c] = -v
        roots = [lax.rsqrt(a[k, k]) for k in range(8)]
        ul, ur = None, None
        for c in range(8):
            m = jnp.where(sub == c, roots[c], 0.0)
            for r in range(c + 1, 8):
                m = jnp.where(sub == r, w[r, c] * roots[r], m)
            tl, tr = m * spread(left[q][c : c + 1, :]), m * spread(right[q][c : c + 1, :])
            ul, ur = (tl, tr) if ul is None else (ul + tl, ur + tr)
        out.append(ur)
        if q == NB // 8 - 1:
            break
        turned = ul.T
        rows_l = [spread(ul[c : c + 1, :]) for c in range(8)]
        rows_r = [spread(ur[c : c + 1, :]) for c in range(8)]
        for p in range(q + 1, NB // 8):
            for c in range(8):
                m = spread(turned[8 * p : 8 * p + 8, c : c + 1])
                left[p] = left[p] - m * rows_l[c]
                right[p] = right[p] - m * rows_r[c]
    return jnp.concatenate(out, axis=0)


def dot32(a, b, dims):
    return lax.dot_general(
        a, b, (dims, ((), ())), precision=lax.Precision.HIGHEST, preferred_element_type=jnp.float32
    )


def finish(snaps, row_count, col_count, where_ref, acc_ref, out_ref):
    t, s = where_ref[0], where_ref[1]
    head = slice(row_count, row_count + NB)

    def gram_part(rows, cols, row_start, col_start):
        value = acc_ref[rows, cols] * (1.0 / snaps)
        row_ids = row_start + lax.broadcasted_iota(jnp.int32, value.shape, 0)
        col_ids = col_start + lax.broadcasted_iota(jnp.int32, value.shape, 1)
        return value + REG * (row_ids == col_ids).astype(jnp.float32), row_ids

    own = slice(NB, NB + col_count)
    inverse = inverse_factor(gram_part(head, slice(0, NB), 0, 0)[0])
    cols_factor = dot32(inverse, gram_part(head, own, 0, s * col_count)[0], ((1,), (0,)))
    for at in range(0, row_count, NB):
        rows = slice(at, min(at + NB, row_count))
        factor = dot32(gram_part(rows, slice(0, NB), t * row_count + at, 0)[0], inverse, ((1,), (1,)))
        value, row_ids = gram_part(rows, own, t * row_count + at, s * col_count)
        value = value - dot32(factor, cols_factor, ((1,), (0,)))
        value = jnp.where(row_ids < NB, 0.0, value)
        out_ref[rows, NB:col_count] = value[:, NB:]
        out_ref[rows, 0:NB] = jnp.where(s == 0, factor, value[:, :NB])


def swap(x, axis, bit):
    return lax.ppermute(x, axis, [(i, i ^ bit) for i in range(lax.axis_size(axis))])


def shards(snapshots, pod_basis, inputs):
    modes = pod_basis.shape[1]
    space_count, time_count = lax.axis_size("space"), lax.axis_size("tm")
    t, s = lax.axis_index("tm"), lax.axis_index("space")
    local = snapshots.shape[1]
    snaps = local * time_count
    depth = local // space_count
    plan = make_plan(modes, inputs.shape[0], time_count, space_count)

    def some(x, bit, wanted):
        pairs = [
            (a * time_count + b, a * time_count + (b ^ bit))
            for a in range(space_count)
            for b in range(time_count)
            if a == space_count - 1 or b in wanted
        ]
        return lax.ppermute(x, ("space", "tm"), pairs)

    u_near = some(inputs, 1, (2,))
    u_far = some(inputs, 2, (0, 1))

    limit = 1200.0 * 0.0625 * snapshots.shape[0] * space_count
    shrink = 2.0 ** -max(0, math.ceil(math.log2(limit / 65000.0)))
    part = jnp.einsum("dr,ds->rs", pod_basis, snapshots, preferred_element_type=jnp.float32)
    part = (part * shrink).astype(jnp.float16)
    part = part.reshape(modes, space_count, depth).transpose(1, 0, 2)
    part = lax.all_to_all(part, "space", 0, 0, tiled=False)
    mine = jnp.sum(part.astype(jnp.float32), axis=0).astype(jnp.float16)[None]
    mine, u_near, u_far = lax.optimization_barrier((mine, u_near, u_far))
    u_far_near = some(u_far, 1, (2,))

    bits = [1 << b for b in reversed(range(space_count.bit_length() - 1))]
    wide = mine[0].astype(jnp.float32)
    energy = jnp.sum(wide * wide, axis=1)
    for axis, bit in [("tm", 2), ("tm", 1)] + [("space", bit) for bit in bits]:
        energy = energy + swap(energy, axis, bit)
    order = [0]
    for bit in bits[:-1]:
        mine = jnp.concatenate([mine, swap(mine, "space", bit)], axis=0)
        order = order + [o ^ bit for o in order]
    inv = (shrink ** -1 / jnp.sqrt(energy / (snaps * shrink * shrink) + EPS))[:, None]
    order = jnp.asarray(order + [o ^ 1 for o in order], jnp.int32)
    where = jnp.concatenate([jnp.stack([t, s]), s ^ order]).astype(jnp.int32)

    def both(x):
        return x.astype(jnp.float32), swap(x, "tm", 1).astype(jnp.float32)

    diagonal = [
        (a * time_count + b, (a ^ 1) * time_count + (b ^ 2)) for a in range(space_count) for b in range(time_count)
    ]
    beside = swap(mine, "space", 1)
    far = swap(mine, "tm", 2)
    cross = lax.ppermute(mine, ("space", "tm"), diagonal)
    us = [inputs, u_near, u_far, u_far_near]
    acc = gram_call(plan, snaps, where, [[x] for x in both(mine)], us[:2], [0, 1], [0, 0], inv)
    acc, beside, far, cross = lax.optimization_barrier((acc, beside, far, cross))
    xs = [[x] for x in both(beside) + both(far) + both(cross)]
    return gram_call(plan, snaps, where, xs, us, [0, 1, 2, 3, 2, 3], [1, 1, 0, 0, 1, 1], inv, acc)


def solution(mesh):
    return jax.shard_map(
        shards,
        mesh=mesh,
        in_specs=(P("space", "tm"), P("space", None), P(None, "tm")),
        out_specs=P("tm", "space"),
        check_vma=False,
    )
```

```python
import functools
import math

import jax
import jax.numpy as jnp
import numpy as np
from jax import lax
from jax.experimental import pallas as pl
from jax.experimental.pallas import tpu as pltpu
from jax.sharding import PartitionSpec as P

NB = 128
EPS = 1e-06
REG = 0.5
PAD = 8
LANES = 128


def feature_pairs(modes, count):
    first, second = np.triu_indices(modes)
    lead = [(f, None) for f in range(modes)]
    pairs = list(zip(first.tolist(), second.tolist()))
    tail = [(modes + k, None) for k in range(count)]
    return lead + pairs + tail


def runs_of(rows):
    runs = []
    for at, row in enumerate(rows):
        if row is None:
            continue
        a, b = row
        key = ("one", a - at) if b is None else (a, b - at)
        if runs and runs[-1][2] == key and runs[-1][1] == at:
            runs[-1][1] = at + 1
        else:
            runs.append([at, at + 1, key])
    return runs


def build_rows(x_ref, f_ref, lane, rows, base):
    sub = lax.broadcasted_iota(jnp.int32, (8, LANES), 0)
    cache = {}

    def row_of(a):
        if a not in cache:
            cache.clear()
            cache[a] = jnp.broadcast_to(x_ref[lane, PAD + a : PAD + a + 1, :], (8, LANES))
        return cache[a]

    def eight(at):
        chunk = rows[at : at + 8]
        chunk = chunk + [None] * (8 - len(chunk))
        total = None
        for lo, hi, (a, shift) in runs_of(chunk):
            part = x_ref[lane, PAD + shift : PAD + shift + 8, :]
            if a != "one":
                part = part * row_of(a)
            if total is None and lo == 0:
                total = part
            else:
                if total is None:
                    total = jnp.zeros((8, LANES), jnp.float32)
                total = jnp.where(sub >= lo, part, total)
            last = hi
        if total is None:
            return jnp.zeros((8, LANES), jnp.float32)
        if last < 8:
            total = jnp.where(sub < last, total, 0.0)
        return total

    for at in range(0, len(rows), 16):
        value = jnp.concatenate([eight(at), eight(at + 8)], axis=0).astype(jnp.bfloat16)
        f_ref[base + at : base + at + 16, pl.ds(pl.multiple_of(lane * LANES, LANES), LANES)] = value


def gram_kernel(plan, snaps, shrink, closing, feed, where_ref, *refs):
    modes, row_sets, col_sets, head_set, row_count, a_rows, b_rows = plan
    pieces, sources, tables = feed
    x_ins, refs = refs[: sum(pieces)], refs[sum(pieces) :]
    u_ins, refs = refs[: max(sources) + 1], refs[max(sources) + 1 :]
    energy_ref, refs = refs[0], refs[1:]
    if closing:
        acc_in, out_ref, acc_ref, acc_sem = refs[:4]
        prior = pltpu.make_async_copy(acc_in, acc_ref, acc_sem)
    else:
        acc_ref = refs[0]
    x_buf, x_sem, u_buf, u_sem, x_ref, f_ref = refs[-6:]
    step, steps = pl.program_id(0), len(pieces)
    _, slots, inputs, slot_depth = u_buf.shape
    per = slot_depth // LANES
    lanes = slots * per
    wanted = jnp.logical_or(where_ref[0] == len(row_sets) - 1, where_ref[1] == len(col_sets) - 1)

    def x_copies(number):
        copies, at = [], 0
        for piece in range(pieces[number]):
            ref = x_ins[sum(pieces[:number]) + piece]
            copies.append(
                pltpu.make_async_copy(ref, x_buf.at[number % 2, at : at + ref.shape[0]], x_sem.at[number % 2, piece])
            )
            at += ref.shape[0]
        return copies

    def u_copies(number):
        for slot in range(slots):
            chunk = where_ref[2 + tables[number] * slots + slot]
            at = pl.ds(pl.multiple_of(chunk * slot_depth, slot_depth), slot_depth)
            yield pltpu.make_async_copy(
                u_ins[sources[number]].at[:, at], u_buf.at[number % 2, slot], u_sem.at[number % 2, slot]
            )

    def fetch(number):
        for copy in x_copies(number):
            copy.start()
        pl.when(wanted)(lambda: [copy.start() for copy in u_copies(number)] and None)

    def arrive(number):
        for copy in x_copies(number):
            copy.wait()
        pl.when(wanted)(lambda: [copy.wait() for copy in u_copies(number)] and None)

    @pl.when(step == 0)
    def _():
        fetch(0)
        if closing:
            prior.start()
        else:
            acc_ref[...] = jnp.zeros_like(acc_ref)

    scale = lax.rsqrt(energy_ref[...] * (1.0 / (snaps * shrink * shrink)) + EPS) * (1.0 / shrink)
    ids = lax.broadcasted_iota(jnp.int32, (modes, modes), 0), lax.broadcasted_iota(jnp.int32, (modes, modes), 1)
    scale = jnp.sum(jnp.where(ids[0] == ids[1], scale, 0.0), axis=1, keepdims=True)
    for number in range(steps):
        @pl.when(step == number)
        def _(number=number):
            if number + 1 < steps:
                fetch(number + 1)
            arrive(number)
            now = number % 2
            for lane in range(lanes):
                at = slice(lane % per * LANES, (lane % per + 1) * LANES)
                x_ref[lane, PAD : PAD + modes, :] = x_buf[now, lane // per, :, at] * scale

            @pl.when(wanted)
            def _():
                for lane in range(lanes):
                    at = slice(lane % per * LANES, (lane % per + 1) * LANES)
                    rows = slice(PAD + modes, PAD + modes + inputs)
                    x_ref[lane, rows, :] = u_buf[now, lane // per, :, at].astype(jnp.float32)

    def build(rows, base):
        @pl.loop(0, lanes)
        def _(lane):
            build_rows(x_ref, f_ref, lane, rows, base)

    for number, rows in enumerate(row_sets):
        pl.when(where_ref[0] == number)(lambda rows=rows: build(rows, 0))
    build(head_set, row_count)
    for number, rows in enumerate(col_sets):
        pl.when(where_ref[1] == number)(lambda rows=rows: build(rows, a_rows))

    if closing:
        pl.when(step == 0)(prior.wait)
    def contract():
        left = f_ref[0:a_rows, :]
        for at in range(0, b_rows, 256):
            wide = min(256, b_rows - at)
            right = f_ref[row_count + at : row_count + at + wide, :]
            acc_ref[:, at : at + wide] += lax.dot_general(
                left, right, (((1,), (1,)), ((), ())), preferred_element_type=jnp.float32
            )

    if not closing:
        contract()
        return
    pl.when(step < steps - 1)(contract)

    @pl.when(step == steps - 1)
    def _():
        head = f_ref[row_count:a_rows, :]
        corner = lax.dot_general(head, head, (((1,), (1,)), ((), ())), preferred_element_type=jnp.float32)
        corner = (acc_ref[row_count:a_rows, 0:NB] + corner) * (1.0 / snaps)
        ids = lax.broadcasted_iota(jnp.int32, (NB, NB), 0), lax.broadcasted_iota(jnp.int32, (NB, NB), 1)
        inverse = inverse_factor(corner + REG * (ids[0] == ids[1]).astype(jnp.float32))
        contract()
        finish(snaps, row_count, len(col_sets[0]), where_ref, inverse, acc_ref, out_ref)


def make_plan(modes, count, time_count, space_count):
    pairs = feature_pairs(modes, count)
    total = len(pairs)
    row_count, col_count = total // time_count, total // space_count
    row_sets = [pairs[t * row_count : (t + 1) * row_count] for t in range(time_count)]
    col_sets = [pairs[s * col_count : (s + 1) * col_count] for s in range(space_count)]
    a_rows = row_count + NB
    b_rows = -(-(NB + col_count) // 128) * 128
    return modes, row_sets, col_sets, pairs[:NB], row_count, a_rows, b_rows


def gram_call(plan, snaps, shrink, where, xs, us, sources, tables, energy, acc=None):
    modes, _, col_sets, _, row_count, a_rows, b_rows = plan
    inputs = us[0].shape[0]
    slot_depth = xs[0][0].shape[2]
    slots = sum(piece.shape[0] for piece in xs[0])
    depth = slots * slot_depth
    lanes = depth // LANES
    steps = len(xs)
    pieces = [len(x) for x in xs]
    closing = acc is not None
    args = [piece for x in xs for piece in x] + list(us)
    in_specs = [pl.BlockSpec(memory_space=pl.ANY)] * len(args)
    args.append(energy)
    in_specs.append(pl.BlockSpec((1, modes), lambda k, w: (0, 0)))
    acc_shape = out_shape = (a_rows, b_rows)
    scratch = [
        pltpu.VMEM((2, slots, modes, slot_depth), jnp.float32),
        pltpu.SemaphoreType.DMA((2, max(pieces))),
        pltpu.VMEM((2, slots, inputs, slot_depth), jnp.bfloat16),
        pltpu.SemaphoreType.DMA((2, slots)),
        pltpu.VMEM((lanes, PAD + modes + inputs + 8, LANES), jnp.float32),
        pltpu.VMEM((-(-(row_count + b_rows) // 16) * 16, depth), jnp.bfloat16),
    ]
    if closing:
        in_specs.append(pl.BlockSpec(memory_space=pl.ANY))
        args.append(acc)
        scratch = [pltpu.VMEM(acc_shape, jnp.float32), pltpu.SemaphoreType.DMA] + scratch
        out_shape = (row_count, len(col_sets[0]))
    flops = 2 * a_rows * b_rows * steps * depth
    return pl.pallas_call(
        functools.partial(gram_kernel, plan, snaps, shrink, closing, (pieces, sources, tables)),
        grid_spec=pltpu.PrefetchScalarGridSpec(
            num_scalar_prefetch=1,
            grid=(steps,),
            in_specs=in_specs,
            out_specs=pl.BlockSpec(out_shape, lambda k, w: (0, 0)),
            scratch_shapes=scratch,
        ),
        out_shape=jax.ShapeDtypeStruct(out_shape, jnp.float32),
        compiler_params=pltpu.CompilerParams(
            vmem_limit_bytes=56 * 1024 * 1024, dimension_semantics=("arbitrary",)
        ),
        cost_estimate=pl.CostEstimate(flops=2 * flops, bytes_accessed=20_000_000, transcendentals=0),
        name="close" if closing else "gram",
    )(where, *args)


def inverse_factor(corner):
    row_ids = lax.broadcasted_iota(jnp.int32, (NB, NB), 0)
    col_ids = lax.broadcasted_iota(jnp.int32, (NB, NB), 1)
    eye = (row_ids == col_ids).astype(jnp.float32)
    sub = lax.broadcasted_iota(jnp.int32, (8, NB), 0)
    left = [corner[at : at + 8] for at in range(0, NB, 8)]
    right = [eye[at : at + 8] for at in range(0, NB, 8)]
    spread = lambda x: jnp.broadcast_to(x, (8, NB))
    out = []
    for q in range(NB // 8):
        columns = [spread(left[q][:, 8 * q + c : 8 * q + c + 1]) for c in range(8)]
        a = {(r, c): spread(columns[c][r : r + 1, :]) for r in range(8) for c in range(r + 1)}
        low = {}
        invd = []
        for k in range(8):
            inv = 1.0 / a[k, k]
            invd.append(inv)
            for r in range(k + 1, 8):
                low[r, k] = a[r, k] * inv
            for r in range(k + 1, 8):
                for c in range(k + 1, r + 1):
                    a[r, c] = a[r, c] - low[r, k] * a[c, k]
            w = {}
        for c in range(8):
            for r in range(c + 1, 8):
                v = low[r, c]
                for m in range(c + 1, r):
                    v = v + low[r, m] * w[m, c]
                w[r, c] = -v
        roots = [lax.rsqrt(a[k, k]) for k in range(8)]
        ul, ur = None, None
        for c in range(8):
            m = jnp.where(sub == c, roots[c], 0.0)
            for r in range(c + 1, 8):
                m = jnp.where(sub == r, w[r, c] * roots[r], m)
            tl, tr = m * spread(left[q][c : c + 1, :]), m * spread(right[q][c : c + 1, :])
            ul, ur = (tl, tr) if ul is None else (ul + tl, ur + tr)
        out.append(ur)
        if q == NB // 8 - 1:
            break
        turned = ul.T
        rows_l = [spread(ul[c : c + 1, :]) for c in range(8)]
        rows_r = [spread(ur[c : c + 1, :]) for c in range(8)]
        for p in range(q + 1, NB // 8):
            for c in range(8):
                m = spread(turned[8 * p : 8 * p + 8, c : c + 1])
                left[p] = left[p] - m * rows_l[c]
                right[p] = right[p] - m * rows_r[c]
    return jnp.concatenate(out, axis=0)


def halves(x):
    high = x.astype(jnp.bfloat16)
    return high, (x - high.astype(jnp.float32)).astype(jnp.bfloat16)


def dot32(a, b):
    (a_high, a_low), (b_high, b_low) = a, b
    both = jnp.dot(
        jnp.concatenate([a_high, a_high], axis=1),
        jnp.concatenate([b_high, b_low], axis=0),
        preferred_element_type=jnp.float32,
    )
    return both + jnp.dot(a_low, b_high, preferred_element_type=jnp.float32)


def finish(snaps, row_count, col_count, where_ref, inverse, acc_ref, out_ref):
    t, s = where_ref[0], where_ref[1]
    head = slice(row_count, row_count + NB)

    def gram_part(rows, cols, row_start, col_start):
        value = acc_ref[rows, cols] * (1.0 / snaps)
        row_ids = row_start + lax.broadcasted_iota(jnp.int32, value.shape, 0)
        col_ids = col_start + lax.broadcasted_iota(jnp.int32, value.shape, 1)
        return value + REG * (row_ids == col_ids).astype(jnp.float32), row_ids

    own = slice(NB, NB + col_count)
    cols_factor = dot32(halves(inverse), halves(gram_part(head, own, 0, s * col_count)[0]))
    cols_factor, turned = halves(cols_factor), halves(inverse.T)
    tall = row_count // 4
    for at in range(0, row_count, tall):
        rows = slice(at, at + tall)
        factor = dot32(halves(gram_part(rows, slice(0, NB), t * row_count + at, 0)[0]), turned)
        value, row_ids = gram_part(rows, own, t * row_count + at, s * col_count)
        value = value - dot32(halves(factor), cols_factor)
        value = jnp.where(row_ids < NB, 0.0, value)
        out_ref[rows, NB:col_count] = value[:, NB:]
        out_ref[rows, 0:NB] = jnp.where(s == 0, factor, value[:, :NB])


def swap(x, axis, bit):
    return lax.ppermute(x, axis, [(i, i ^ bit) for i in range(lax.axis_size(axis))])


def shards(snapshots, pod_basis, inputs):
    modes = pod_basis.shape[1]
    space_count, time_count = lax.axis_size("space"), lax.axis_size("tm")
    t, s = lax.axis_index("tm"), lax.axis_index("space")
    local = snapshots.shape[1]
    snaps = local * time_count
    depth = local // space_count
    plan = make_plan(modes, inputs.shape[0], time_count, space_count)

    def some(x, bit, wanted):
        pairs = [
            (a * time_count + b, a * time_count + (b ^ bit))
            for a in range(space_count)
            for b in range(time_count)
            if a == space_count - 1 or b in wanted
        ]
        return lax.ppermute(x, ("space", "tm"), pairs)

    u_near = some(inputs, 1, (2,))
    u_far = some(inputs, 2, (0, 1))

    limit = 1200.0 * 0.0625 * snapshots.shape[0] * space_count
    shrink = 2.0 ** -max(0, math.ceil(math.log2(limit / 65000.0)))
    part = jnp.einsum("dr,ds->rs", pod_basis, snapshots, preferred_element_type=jnp.float32)
    part = (part * shrink).astype(jnp.float16)
    part = part.reshape(modes, space_count, depth).transpose(1, 0, 2)
    part = lax.all_to_all(part, "space", 0, 0, tiled=False)
    mine = jnp.sum(part.astype(jnp.float32), axis=0).astype(jnp.float16)[None]
    mine, u_near = lax.optimization_barrier((mine, u_near))

    def partners(axes):
        return [a ^ b for a in (0, axes[0]) for b in (0, axes[-1])][1:] if len(axes) > 1 else axes

    def crossing(a_bit, b_bit):
        return [
            (a * time_count + b, (a ^ a_bit) * time_count + (b ^ b_bit))
            for a in range(space_count)
            for b in range(time_count)
        ]

    bits = [1 << b for b in reversed(range(1, space_count.bit_length() - 1))]
    levels = [bits[at : at + 2] for at in range(0, len(bits), 2)]
    order = [0]
    for level in levels:
        mine = jnp.concatenate([mine] + [swap(mine, "space", bit) for bit in partners(level)], axis=0)
        order = order + [o ^ bit for bit in partners(level) for o in order]
    mine, u_far = lax.optimization_barrier((mine, u_far))
    wide = mine.astype(jnp.float32)
    energy = jnp.sum(wide * wide, axis=(0, 2))[None]
    moves = [(0, 2), (1, 0), (1, 2)]
    energy = energy + sum(lax.ppermute(energy, ("space", "tm"), crossing(*move)) for move in moves)
    energy = energy + swap(energy, "tm", 1)
    mine, energy = lax.optimization_barrier((mine, energy))
    order = jnp.asarray(order + [o ^ 1 for o in order], jnp.int32)
    where = jnp.concatenate([jnp.stack([t, s]), s ^ order]).astype(jnp.int32)

    def both(x):
        x = x.astype(jnp.float32)
        return x, swap(x, "tm", 1)

    beside = swap(mine, "space", 1)
    far = swap(mine, "tm", 2)
    cross = lax.ppermute(mine, ("space", "tm"), crossing(1, 2))
    us = [inputs, u_near]
    acc = gram_call(plan, snaps, shrink, where, [[x] for x in both(mine)], us, [0, 1], [0, 0], energy)
    acc, beside, far, cross, u_far = lax.optimization_barrier((acc, beside, far, cross, u_far))
    us = us + [u_far, some(u_far, 1, (2,))]
    xs = [[x] for x in both(beside) + both(far) + both(cross)]
    return gram_call(plan, snaps, shrink, where, xs, us, [0, 1, 2, 3, 2, 3], [1, 1, 0, 0, 1, 1], energy, acc)


def solution(mesh):
    return jax.shard_map(
        shards,
        mesh=mesh,
        in_specs=(P("space", "tm"), P("space", None), P(None, "tm")),
        out_specs=P("tm", "space"),
        check_vma=False,
    )
```

```python
import functools
import math

import jax
import jax.numpy as jnp
import numpy as np
from jax import lax
from jax.experimental import pallas as pl
from jax.experimental.pallas import tpu as pltpu
from jax.sharding import PartitionSpec as P

NB = 128
EPS = 1e-06
REG = 0.5
PAD = 8
LANES = 128


def feature_pairs(modes, count):
    first, second = np.triu_indices(modes)
    lead = [(f, None) for f in range(modes)]
    pairs = list(zip(first.tolist(), second.tolist()))
    tail = [(modes + k, None) for k in range(count)]
    return lead + pairs + tail


def runs_of(rows):
    runs = []
    for at, row in enumerate(rows):
        if row is None:
            continue
        a, b = row
        key = ("one", a - at) if b is None else (a, b - at)
        if runs and runs[-1][2] == key and runs[-1][1] == at:
            runs[-1][1] = at + 1
        else:
            runs.append([at, at + 1, key])
    return runs


def build_rows(x_ref, f_ref, lane, rows, base):
    sub = lax.broadcasted_iota(jnp.int32, (8, LANES), 0)
    cache = {}

    def row_of(a):
        if a not in cache:
            cache.clear()
            cache[a] = jnp.broadcast_to(x_ref[lane, PAD + a : PAD + a + 1, :], (8, LANES))
        return cache[a]

    def eight(at):
        chunk = rows[at : at + 8]
        chunk = chunk + [None] * (8 - len(chunk))
        total = None
        for lo, hi, (a, shift) in runs_of(chunk):
            part = x_ref[lane, PAD + shift : PAD + shift + 8, :]
            if a != "one":
                part = part * row_of(a)
            if total is None and lo == 0:
                total = part
            else:
                if total is None:
                    total = jnp.zeros((8, LANES), jnp.float32)
                total = jnp.where(sub >= lo, part, total)
            last = hi
        if total is None:
            return jnp.zeros((8, LANES), jnp.float32)
        if last < 8:
            total = jnp.where(sub < last, total, 0.0)
        return total

    for at in range(0, len(rows), 16):
        value = jnp.concatenate([eight(at), eight(at + 8)], axis=0)
        f_ref[base + at : base + at + 16, pl.ds(pl.multiple_of(lane * LANES, LANES), LANES)] = value


def gram_kernel(plan, snaps, shrink, closing, feed, where_ref, *refs):
    modes, row_sets, col_sets, head_set, row_count, a_rows, b_rows = plan
    pieces, sources, tables = feed
    x_ins, refs = refs[: sum(pieces)], refs[sum(pieces) :]
    u_ins, refs = refs[: max(sources) + 1], refs[max(sources) + 1 :]
    energy_refs, refs = refs[:4], refs[4:]
    if closing:
        acc_in, out_ref, acc_ref, acc_sem = refs[:4]
        prior = pltpu.make_async_copy(acc_in, acc_ref, acc_sem)
    else:
        acc_ref = refs[0]
    x_buf, x_sem, u_buf, u_sem, x_ref, f_ref = refs[-6:]
    step, steps = pl.program_id(0), len(pieces)
    _, slots, inputs, slot_depth = u_buf.shape
    per = slot_depth // LANES
    lanes = slots * per
    wanted = jnp.logical_or(where_ref[0] == len(row_sets) - 1, where_ref[1] == len(col_sets) - 1)

    def x_copies(number):
        copies, at = [], 0
        for piece in range(pieces[number]):
            ref = x_ins[sum(pieces[:number]) + piece]
            copies.append(
                pltpu.make_async_copy(ref, x_buf.at[number % 2, at : at + ref.shape[0]], x_sem.at[number % 2, piece])
            )
            at += ref.shape[0]
        return copies

    def u_copies(number):
        for slot in range(slots):
            chunk = where_ref[2 + tables[number] * slots + slot]
            at = pl.ds(pl.multiple_of(chunk * slot_depth, slot_depth), slot_depth)
            yield pltpu.make_async_copy(
                u_ins[sources[number]].at[:, at], u_buf.at[number % 2, slot], u_sem.at[number % 2, slot]
            )

    def fetch(number):
        for copy in x_copies(number):
            copy.start()
        pl.when(wanted)(lambda: [copy.start() for copy in u_copies(number)] and None)

    def arrive(number):
        for copy in x_copies(number):
            copy.wait()
        pl.when(wanted)(lambda: [copy.wait() for copy in u_copies(number)] and None)

    @pl.when(step == 0)
    def _():
        fetch(0)
        if closing:
            prior.start()
        else:
            acc_ref[...] = jnp.zeros_like(acc_ref)

    energy = sum(ref[...] for ref in energy_refs)
    scale = lax.rsqrt(energy * (1.0 / (snaps * shrink * shrink)) + EPS) * (1.0 / shrink)
    ids = lax.broadcasted_iota(jnp.int32, (modes, modes), 0), lax.broadcasted_iota(jnp.int32, (modes, modes), 1)
    scale = jnp.sum(jnp.where(ids[0] == ids[1], scale, 0.0), axis=1, keepdims=True)
    for number in range(steps):
        @pl.when(step == number)
        def _(number=number):
            if number + 1 < steps:
                fetch(number + 1)
            arrive(number)
            now = number % 2
            for lane in range(lanes):
                at = slice(lane % per * LANES, (lane % per + 1) * LANES)
                x_ref[lane, PAD : PAD + modes, :] = x_buf[now, lane // per, :, at] * scale

            @pl.when(wanted)
            def _():
                for lane in range(lanes):
                    at = slice(lane % per * LANES, (lane % per + 1) * LANES)
                    rows = slice(PAD + modes, PAD + modes + inputs)
                    x_ref[lane, rows, :] = u_buf[now, lane // per, :, at].astype(jnp.float32)

    def build(rows, base):
        @pl.loop(0, lanes)
        def _(lane):
            build_rows(x_ref, f_ref, lane, rows, base)

    for number, rows in enumerate(row_sets):
        pl.when(where_ref[0] == number)(lambda rows=rows: build(rows, 0))
    build(head_set, row_count)
    for number, rows in enumerate(col_sets):
        pl.when(where_ref[1] == number)(lambda rows=rows: build(rows, a_rows))

    if closing:
        pl.when(step == 0)(prior.wait)
    def contract():
        left = f_ref[0:a_rows, :]
        for at in range(0, b_rows, 256):
            wide = min(256, b_rows - at)
            right = f_ref[row_count + at : row_count + at + wide, :]
            acc_ref[:, at : at + wide] += lax.dot_general(
                left, right, (((1,), (1,)), ((), ())), preferred_element_type=jnp.float32
            )

    if not closing:
        contract()
        return
    pl.when(step < steps - 1)(contract)

    @pl.when(step == steps - 1)
    def _():
        head = f_ref[row_count:a_rows, :]
        corner = lax.dot_general(head, head, (((1,), (1,)), ((), ())), preferred_element_type=jnp.float32)
        corner = (acc_ref[row_count:a_rows, 0:NB] + corner) * (1.0 / snaps)
        ids = lax.broadcasted_iota(jnp.int32, (NB, NB), 0), lax.broadcasted_iota(jnp.int32, (NB, NB), 1)
        inverse = inverse_factor(corner + REG * (ids[0] == ids[1]).astype(jnp.float32))
        contract()
        finish(snaps, row_count, len(col_sets[0]), where_ref, inverse, acc_ref, out_ref)


def make_plan(modes, count, time_count, space_count):
    pairs = feature_pairs(modes, count)
    total = len(pairs)
    row_count, col_count = total // time_count, total // space_count
    row_sets = [pairs[t * row_count : (t + 1) * row_count] for t in range(time_count)]
    col_sets = [pairs[s * col_count : (s + 1) * col_count] for s in range(space_count)]
    a_rows = row_count + NB
    b_rows = -(-(NB + col_count) // 128) * 128
    return modes, row_sets, col_sets, pairs[:NB], row_count, a_rows, b_rows


def gram_call(plan, snaps, shrink, where, xs, us, sources, tables, energy, acc=None):
    modes, _, col_sets, _, row_count, a_rows, b_rows = plan
    inputs = us[0].shape[0]
    slot_depth = xs[0][0].shape[2]
    slots = sum(piece.shape[0] for piece in xs[0])
    depth = slots * slot_depth
    lanes = depth // LANES
    steps = len(xs)
    pieces = [len(x) for x in xs]
    closing = acc is not None
    args = [piece for x in xs for piece in x] + list(us)
    in_specs = [pl.BlockSpec(memory_space=pl.ANY)] * len(args)
    args += energy
    in_specs += [pl.BlockSpec((1, modes), lambda k, w: (0, 0))] * 4
    acc_shape = out_shape = (a_rows, b_rows)
    scratch = [
        pltpu.VMEM((2, slots, modes, slot_depth), jnp.float32),
        pltpu.SemaphoreType.DMA((2, max(pieces))),
        pltpu.VMEM((2, slots, inputs, slot_depth), jnp.bfloat16),
        pltpu.SemaphoreType.DMA((2, slots)),
        pltpu.VMEM((lanes, PAD + modes + inputs + 8, LANES), jnp.float32),
        pltpu.VMEM((-(-(row_count + b_rows) // 16) * 16, depth), jnp.float32),
    ]
    if closing:
        in_specs.append(pl.BlockSpec(memory_space=pl.ANY))
        args.append(acc)
        scratch = [pltpu.VMEM(acc_shape, jnp.float32), pltpu.SemaphoreType.DMA] + scratch
        out_shape = (row_count, len(col_sets[0]))
    flops = 2 * a_rows * b_rows * steps * depth
    return pl.pallas_call(
        functools.partial(gram_kernel, plan, snaps, shrink, closing, (pieces, sources, tables)),
        grid_spec=pltpu.PrefetchScalarGridSpec(
            num_scalar_prefetch=1,
            grid=(steps,),
            in_specs=in_specs,
            out_specs=pl.BlockSpec(out_shape, lambda k, w: (0, 0)),
            scratch_shapes=scratch,
        ),
        out_shape=jax.ShapeDtypeStruct(out_shape, jnp.float32),
        compiler_params=pltpu.CompilerParams(
            vmem_limit_bytes=40 * 1024 * 1024, dimension_semantics=("arbitrary",)
        ),
        cost_estimate=pl.CostEstimate(flops=2 * flops, bytes_accessed=20_000_000, transcendentals=0),
        name="close" if closing else "gram",
    )(where, *args)


def inverse_factor(corner):
    row_ids = lax.broadcasted_iota(jnp.int32, (NB, NB), 0)
    col_ids = lax.broadcasted_iota(jnp.int32, (NB, NB), 1)
    eye = (row_ids == col_ids).astype(jnp.float32)
    sub = lax.broadcasted_iota(jnp.int32, (8, NB), 0)
    left = [corner[at : at + 8] for at in range(0, NB, 8)]
    right = [eye[at : at + 8] for at in range(0, NB, 8)]
    spread = lambda x: jnp.broadcast_to(x, (8, NB))
    out = []
    for q in range(NB // 8):
        columns = [spread(left[q][:, 8 * q + c : 8 * q + c + 1]) for c in range(8)]
        a = {(r, c): spread(columns[c][r : r + 1, :]) for r in range(8) for c in range(r + 1)}
        low = {}
        invd = []
        for k in range(8):
            inv = 1.0 / a[k, k]
            invd.append(inv)
            for r in range(k + 1, 8):
                low[r, k] = a[r, k] * inv
            for r in range(k + 1, 8):
                for c in range(k + 1, r + 1):
                    a[r, c] = a[r, c] - low[r, k] * a[c, k]
            w = {}
        for c in range(8):
            for r in range(c + 1, 8):
                v = low[r, c]
                for m in range(c + 1, r):
                    v = v + low[r, m] * w[m, c]
                w[r, c] = -v
        roots = [lax.rsqrt(a[k, k]) for k in range(8)]
        ul, ur = None, None
        for c in range(8):
            m = jnp.where(sub == c, roots[c], 0.0)
            for r in range(c + 1, 8):
                m = jnp.where(sub == r, w[r, c] * roots[r], m)
            tl, tr = m * spread(left[q][c : c + 1, :]), m * spread(right[q][c : c + 1, :])
            ul, ur = (tl, tr) if ul is None else (ul + tl, ur + tr)
        out.append(ur)
        if q == NB // 8 - 1:
            break
        turned = ul.T
        rows_l = [spread(ul[c : c + 1, :]) for c in range(8)]
        rows_r = [spread(ur[c : c + 1, :]) for c in range(8)]
        for p in range(q + 1, NB // 8):
            for c in range(8):
                m = spread(turned[8 * p : 8 * p + 8, c : c + 1])
                left[p] = left[p] - m * rows_l[c]
                right[p] = right[p] - m * rows_r[c]
    return jnp.concatenate(out, axis=0)


def halves(x):
    high = x.astype(jnp.bfloat16)
    return high, (x - high.astype(jnp.float32)).astype(jnp.bfloat16)


def dot32(a, b):
    (a_high, a_low), (b_high, b_low) = a, b
    both = jnp.dot(
        jnp.concatenate([a_high, a_high], axis=1),
        jnp.concatenate([b_high, b_low], axis=0),
        preferred_element_type=jnp.float32,
    )
    return both + jnp.dot(a_low, b_high, preferred_element_type=jnp.float32)


def finish(snaps, row_count, col_count, where_ref, inverse, acc_ref, out_ref):
    t, s = where_ref[0], where_ref[1]
    head = slice(row_count, row_count + NB)

    def gram_part(rows, cols, row_start, col_start):
        value = acc_ref[rows, cols] * (1.0 / snaps)
        row_ids = row_start + lax.broadcasted_iota(jnp.int32, value.shape, 0)
        col_ids = col_start + lax.broadcasted_iota(jnp.int32, value.shape, 1)
        return value + REG * (row_ids == col_ids).astype(jnp.float32), row_ids

    own = slice(NB, NB + col_count)
    cols_factor = dot32(halves(inverse), halves(gram_part(head, own, 0, s * col_count)[0]))
    cols_factor, turned = halves(cols_factor), halves(inverse.T)
    tall = row_count // 4
    for at in range(0, row_count, tall):
        rows = slice(at, at + tall)
        factor = dot32(halves(gram_part(rows, slice(0, NB), t * row_count + at, 0)[0]), turned)
        value, row_ids = gram_part(rows, own, t * row_count + at, s * col_count)
        value = value - dot32(halves(factor), cols_factor)
        value = jnp.where(row_ids < NB, 0.0, value)
        out_ref[rows, NB:col_count] = value[:, NB:]
        out_ref[rows, 0:NB] = jnp.where(s == 0, factor, value[:, :NB])


def swap(x, axis, bit):
    return lax.ppermute(x, axis, [(i, i ^ bit) for i in range(lax.axis_size(axis))])


def shards(snapshots, pod_basis, inputs):
    modes = pod_basis.shape[1]
    space_count, time_count = lax.axis_size("space"), lax.axis_size("tm")
    t, s = lax.axis_index("tm"), lax.axis_index("space")
    local = snapshots.shape[1]
    snaps = local * time_count
    depth = local // space_count
    plan = make_plan(modes, inputs.shape[0], time_count, space_count)

    def some(x, bit, wanted):
        pairs = [
            (a * time_count + b, a * time_count + (b ^ bit))
            for a in range(space_count)
            for b in range(time_count)
            if a == space_count - 1 or b in wanted
        ]
        return lax.ppermute(x, ("space", "tm"), pairs)

    u_near = some(inputs, 1, (2,))
    u_far = some(inputs, 2, (0, 1))

    limit = 1200.0 * 0.0625 * snapshots.shape[0] * space_count
    shrink = 2.0 ** -max(0, math.ceil(math.log2(limit / 65000.0)))
    part = jnp.einsum("dr,ds->rs", pod_basis, snapshots, preferred_element_type=jnp.float32)
    part = (part * shrink).astype(jnp.float16)
    part = part.reshape(modes, space_count, depth).transpose(1, 0, 2)
    part = lax.all_to_all(part, "space", 0, 0, tiled=False)
    mine = jnp.sum(part.astype(jnp.float32), axis=0).astype(jnp.float16)[None]

    def partners(axes):
        return [a ^ b for a in (0, axes[0]) for b in (0, axes[-1])][1:] if len(axes) > 1 else axes

    def crossing(a_bit, b_bit):
        return [
            (a * time_count + b, (a ^ a_bit) * time_count + (b ^ b_bit))
            for a in range(space_count)
            for b in range(time_count)
        ]

    bits = [1 << b for b in reversed(range(1, space_count.bit_length() - 1))]
    levels = [bits[at : at + 2] for at in range(0, len(bits), 2)]
    order = [0]
    for level in levels:
        order = order + [o ^ bit for bit in partners(level) for o in order]
    order = jnp.asarray(order + [o ^ 1 for o in order], jnp.int32)
    where = jnp.concatenate([jnp.stack([t, s]), s ^ order]).astype(jnp.int32)
    mine, u_near, where = lax.optimization_barrier((mine, u_near, where))
    for level in levels:
        mine = jnp.concatenate([mine] + [swap(mine, "space", bit) for bit in partners(level)], axis=0)
    mine, u_far = lax.optimization_barrier((mine, u_far))
    wide = mine.astype(jnp.float32)
    energy = jnp.sum(wide * wide, axis=(0, 2))[None]
    moves = [(0, 2), (1, 0), (1, 2)]
    energy = energy + swap(energy, "tm", 1)
    energy = [energy] + [lax.ppermute(energy, ("space", "tm"), crossing(*move)) for move in moves]
    mine, energy = lax.optimization_barrier((mine, energy))

    def both(x):
        x = x.astype(jnp.float32)
        return x, swap(x, "tm", 1)

    beside = swap(mine, "space", 1)
    far = swap(mine, "tm", 2)
    cross = lax.ppermute(mine, ("space", "tm"), crossing(1, 2))
    us = [inputs, u_near]
    acc = gram_call(plan, snaps, shrink, where, [[x] for x in both(mine)], us, [0, 1], [0, 0], energy)
    acc, beside, far, cross, u_far = lax.optimization_barrier((acc, beside, far, cross, u_far))
    us = us + [u_far, some(u_far, 1, (2,))]
    xs = [[x] for x in both(beside) + both(far) + both(cross)]
    return gram_call(plan, snaps, shrink, where, xs, us, [0, 1, 2, 3, 2, 3], [1, 1, 0, 0, 1, 1], energy, acc)


def solution(mesh):
    return jax.shard_map(
        shards,
        mesh=mesh,
        in_specs=(P("space", "tm"), P("space", None), P(None, "tm")),
        out_specs=P("tm", "space"),
        check_vma=False,
    )
```

```python
import functools
import math

import jax
import jax.numpy as jnp
import numpy as np
from jax import lax
from jax.experimental import pallas as pl
from jax.experimental.pallas import tpu as pltpu
from jax.sharding import PartitionSpec as P

NB = 128
EPS = 1e-06
REG = 0.5
PAD = 8
LANES = 128


def feature_pairs(modes, count):
    first, second = np.triu_indices(modes)
    lead = [(f, None) for f in range(modes)]
    pairs = list(zip(first.tolist(), second.tolist()))
    tail = [(modes + k, None) for k in range(count)]
    return lead + pairs + tail


def runs_of(rows):
    runs = []
    for at, row in enumerate(rows):
        if row is None:
            continue
        a, b = row
        key = ("one", a - at) if b is None else (a, b - at)
        if runs and runs[-1][2] == key and runs[-1][1] == at:
            runs[-1][1] = at + 1
        else:
            runs.append([at, at + 1, key])
    return runs


def build_rows(x_ref, f_ref, lane, rows, base):
    sub = lax.broadcasted_iota(jnp.int32, (8, LANES), 0)
    cache = {}

    def row_of(a):
        if a not in cache:
            cache.clear()
            cache[a] = jnp.broadcast_to(x_ref[lane, PAD + a : PAD + a + 1, :], (8, LANES))
        return cache[a]

    def eight(at):
        chunk = rows[at : at + 8]
        chunk = chunk + [None] * (8 - len(chunk))
        total = None
        for lo, hi, (a, shift) in runs_of(chunk):
            part = x_ref[lane, PAD + shift : PAD + shift + 8, :]
            if a != "one":
                part = part * row_of(a)
            if total is None and lo == 0:
                total = part
            else:
                if total is None:
                    total = jnp.zeros((8, LANES), jnp.float32)
                total = jnp.where(sub >= lo, part, total)
            last = hi
        if total is None:
            return jnp.zeros((8, LANES), jnp.float32)
        if last < 8:
            total = jnp.where(sub < last, total, 0.0)
        return total

    for at in range(0, len(rows), 16):
        value = jnp.concatenate([eight(at), eight(at + 8)], axis=0)
        f_ref[base + at : base + at + 16, pl.ds(pl.multiple_of(lane * LANES, LANES), LANES)] = value


def gram_kernel(plan, snaps, shrink, closing, feed, where_ref, *refs):
    modes, row_sets, col_sets, head_set, row_count, a_rows, b_rows = plan
    pieces, sources, tables = feed
    x_ins, refs = refs[: sum(pieces)], refs[sum(pieces) :]
    u_ins, refs = refs[: max(sources) + 1], refs[max(sources) + 1 :]
    energy_refs, refs = refs[:4], refs[4:]
    if closing:
        acc_in, out_ref, acc_ref, acc_sem = refs[:4]
        prior = pltpu.make_async_copy(acc_in, acc_ref, acc_sem)
    else:
        acc_ref = refs[0]
    x_buf, x_sem, u_buf, u_sem, x_ref, f_ref = refs[-6:]
    step, steps = pl.program_id(0), len(pieces)
    _, slots, inputs, slot_depth = u_buf.shape
    per = slot_depth // LANES
    lanes = slots * per
    wanted = jnp.logical_or(where_ref[0] == len(row_sets) - 1, where_ref[1] == len(col_sets) - 1)

    def x_copies(number):
        copies, at = [], 0
        for piece in range(pieces[number]):
            ref = x_ins[sum(pieces[:number]) + piece]
            copies.append(
                pltpu.make_async_copy(ref, x_buf.at[number % 2, at : at + ref.shape[0]], x_sem.at[number % 2, piece])
            )
            at += ref.shape[0]
        return copies

    def u_copies(number):
        for slot in range(slots):
            chunk = where_ref[2 + tables[number] * slots + slot]
            at = pl.ds(pl.multiple_of(chunk * slot_depth, slot_depth), slot_depth)
            yield pltpu.make_async_copy(
                u_ins[sources[number]].at[:, at], u_buf.at[number % 2, slot], u_sem.at[number % 2, slot]
            )

    def fetch(number):
        for copy in x_copies(number):
            copy.start()
        pl.when(wanted)(lambda: [copy.start() for copy in u_copies(number)] and None)

    def arrive(number):
        for copy in x_copies(number):
            copy.wait()
        pl.when(wanted)(lambda: [copy.wait() for copy in u_copies(number)] and None)

    @pl.when(step == 0)
    def _():
        fetch(0)
        if closing:
            prior.start()
        else:
            acc_ref[...] = jnp.zeros_like(acc_ref)

    energy = sum(ref[...] for ref in energy_refs)
    scale = lax.rsqrt(energy * (1.0 / (snaps * shrink * shrink)) + EPS) * (1.0 / shrink)
    ids = lax.broadcasted_iota(jnp.int32, (modes, modes), 0), lax.broadcasted_iota(jnp.int32, (modes, modes), 1)
    scale = jnp.sum(jnp.where(ids[0] == ids[1], scale, 0.0), axis=1, keepdims=True)
    for number in range(steps):
        @pl.when(step == number)
        def _(number=number):
            if number + 1 < steps:
                fetch(number + 1)
            arrive(number)
            now = number % 2
            for lane in range(lanes):
                at = slice(lane % per * LANES, (lane % per + 1) * LANES)
                x_ref[lane, PAD : PAD + modes, :] = x_buf[now, lane // per, :, at] * scale

            @pl.when(wanted)
            def _():
                for lane in range(lanes):
                    at = slice(lane % per * LANES, (lane % per + 1) * LANES)
                    rows = slice(PAD + modes, PAD + modes + inputs)
                    x_ref[lane, rows, :] = u_buf[now, lane // per, :, at].astype(jnp.float32)

    def build(rows, base):
        @pl.loop(0, lanes)
        def _(lane):
            build_rows(x_ref, f_ref, lane, rows, base)

    for number, rows in enumerate(row_sets):
        pl.when(where_ref[0] == number)(lambda rows=rows: build(rows, 0))
    build(head_set, row_count)
    for number, rows in enumerate(col_sets):
        pl.when(where_ref[1] == number)(lambda rows=rows: build(rows, a_rows))

    if closing:
        pl.when(step == 0)(prior.wait)
    def contract():
        left = f_ref[0:a_rows, :]
        for at in range(0, b_rows, 256):
            wide = min(256, b_rows - at)
            right = f_ref[row_count + at : row_count + at + wide, :]
            acc_ref[:, at : at + wide] += lax.dot_general(
                left, right, (((1,), (1,)), ((), ())), preferred_element_type=jnp.float32
            )

    if not closing:
        contract()
        return
    pl.when(step < steps - 1)(contract)

    @pl.when(step == steps - 1)
    def _():
        head = f_ref[row_count:a_rows, :]
        corner = lax.dot_general(head, head, (((1,), (1,)), ((), ())), preferred_element_type=jnp.float32)
        corner = (acc_ref[row_count:a_rows, 0:NB] + corner) * (1.0 / snaps)
        ids = lax.broadcasted_iota(jnp.int32, (NB, NB), 0), lax.broadcasted_iota(jnp.int32, (NB, NB), 1)
        inverse = inverse_factor(corner + REG * (ids[0] == ids[1]).astype(jnp.float32))
        contract()
        finish(snaps, row_count, len(col_sets[0]), where_ref, inverse, acc_ref, out_ref)


def make_plan(modes, count, time_count, space_count):
    pairs = feature_pairs(modes, count)
    total = len(pairs)
    row_count, col_count = total // time_count, total // space_count
    row_sets = [pairs[t * row_count : (t + 1) * row_count] for t in range(time_count)]
    col_sets = [pairs[s * col_count : (s + 1) * col_count] for s in range(space_count)]
    a_rows = row_count + NB
    b_rows = -(-(NB + col_count) // 128) * 128
    return modes, row_sets, col_sets, pairs[:NB], row_count, a_rows, b_rows


def gram_call(plan, snaps, shrink, where, xs, us, sources, tables, energy, acc=None):
    modes, _, col_sets, _, row_count, a_rows, b_rows = plan
    inputs = us[0].shape[0]
    slot_depth = xs[0][0].shape[2]
    slots = sum(piece.shape[0] for piece in xs[0])
    depth = slots * slot_depth
    lanes = depth // LANES
    steps = len(xs)
    pieces = [len(x) for x in xs]
    closing = acc is not None
    args = [piece for x in xs for piece in x] + list(us)
    in_specs = [pl.BlockSpec(memory_space=pl.ANY)] * len(args)
    args += energy
    in_specs += [pl.BlockSpec((1, modes), lambda k, w: (0, 0))] * 4
    acc_shape = out_shape = (a_rows, b_rows)
    scratch = [
        pltpu.VMEM((2, slots, modes, slot_depth), jnp.float32),
        pltpu.SemaphoreType.DMA((2, max(pieces))),
        pltpu.VMEM((2, slots, inputs, slot_depth), jnp.bfloat16),
        pltpu.SemaphoreType.DMA((2, slots)),
        pltpu.VMEM((lanes, PAD + modes + inputs + 8, LANES), jnp.float32),
        pltpu.VMEM((-(-(row_count + b_rows) // 16) * 16, depth), jnp.float32),
    ]
    if closing:
        in_specs.append(pl.BlockSpec(memory_space=pl.ANY))
        args.append(acc)
        scratch = [pltpu.VMEM(acc_shape, jnp.float32), pltpu.SemaphoreType.DMA] + scratch
        out_shape = (row_count, len(col_sets[0]))
    flops = 2 * a_rows * b_rows * steps * depth
    return pl.pallas_call(
        functools.partial(gram_kernel, plan, snaps, shrink, closing, (pieces, sources, tables)),
        grid_spec=pltpu.PrefetchScalarGridSpec(
            num_scalar_prefetch=1,
            grid=(steps,),
            in_specs=in_specs,
            out_specs=pl.BlockSpec(out_shape, lambda k, w: (0, 0)),
            scratch_shapes=scratch,
        ),
        out_shape=jax.ShapeDtypeStruct(out_shape, jnp.float32),
        compiler_params=pltpu.CompilerParams(
            vmem_limit_bytes=40 * 1024 * 1024, dimension_semantics=("arbitrary",)
        ),
        cost_estimate=pl.CostEstimate(flops=2 * flops, bytes_accessed=20_000_000, transcendentals=0),
        name="close" if closing else "gram",
    )(where, *args)


def inverse_factor(corner):
    row_ids = lax.broadcasted_iota(jnp.int32, (NB, NB), 0)
    col_ids = lax.broadcasted_iota(jnp.int32, (NB, NB), 1)
    eye = (row_ids == col_ids).astype(jnp.float32)
    sub = lax.broadcasted_iota(jnp.int32, (8, NB), 0)
    left = [corner[at : at + 8] for at in range(0, NB, 8)]
    right = [eye[at : at + 8] for at in range(0, NB, 8)]
    spread = lambda x: jnp.broadcast_to(x, (8, NB))
    out = []
    for q in range(NB // 8):
        columns = [spread(left[q][:, 8 * q + c : 8 * q + c + 1]) for c in range(8)]
        a = {(r, c): spread(columns[c][r : r + 1, :]) for r in range(8) for c in range(r + 1)}
        low = {}
        invd = []
        for k in range(8):
            inv = 1.0 / a[k, k]
            invd.append(inv)
            for r in range(k + 1, 8):
                low[r, k] = a[r, k] * inv
            for r in range(k + 1, 8):
                for c in range(k + 1, r + 1):
                    a[r, c] = a[r, c] - low[r, k] * a[c, k]
            w = {}
        for c in range(8):
            for r in range(c + 1, 8):
                v = low[r, c]
                for m in range(c + 1, r):
                    v = v + low[r, m] * w[m, c]
                w[r, c] = -v
        roots = [lax.rsqrt(a[k, k]) for k in range(8)]
        ul, ur = None, None
        for c in range(8):
            m = jnp.where(sub == c, roots[c], 0.0)
            for r in range(c + 1, 8):
                m = jnp.where(sub == r, w[r, c] * roots[r], m)
            tl, tr = m * spread(left[q][c : c + 1, :]), m * spread(right[q][c : c + 1, :])
            ul, ur = (tl, tr) if ul is None else (ul + tl, ur + tr)
        out.append(ur)
        if q == NB // 8 - 1:
            break
        turned = ul.T
        rows_l = [spread(ul[c : c + 1, :]) for c in range(8)]
        rows_r = [spread(ur[c : c + 1, :]) for c in range(8)]
        for p in range(q + 1, NB // 8):
            for c in range(8):
                m = spread(turned[8 * p : 8 * p + 8, c : c + 1])
                left[p] = left[p] - m * rows_l[c]
                right[p] = right[p] - m * rows_r[c]
    return jnp.concatenate(out, axis=0)


def halves(x):
    high = x.astype(jnp.bfloat16)
    return high, (x - high.astype(jnp.float32)).astype(jnp.bfloat16)


def dot32(a, b):
    (a_high, a_low), (b_high, b_low) = a, b
    both = jnp.dot(
        jnp.concatenate([a_high, a_high], axis=1),
        jnp.concatenate([b_high, b_low], axis=0),
        preferred_element_type=jnp.float32,
    )
    return both + jnp.dot(a_low, b_high, preferred_element_type=jnp.float32)


def finish(snaps, row_count, col_count, where_ref, inverse, acc_ref, out_ref):
    t, s = where_ref[0], where_ref[1]
    head = slice(row_count, row_count + NB)

    def gram_part(rows, cols, row_start, col_start):
        value = acc_ref[rows, cols] * (1.0 / snaps)
        row_ids = row_start + lax.broadcasted_iota(jnp.int32, value.shape, 0)
        col_ids = col_start + lax.broadcasted_iota(jnp.int32, value.shape, 1)
        return value + REG * (row_ids == col_ids).astype(jnp.float32), row_ids

    own = slice(NB, NB + col_count)
    cols_factor = dot32(halves(inverse), halves(gram_part(head, own, 0, s * col_count)[0]))
    cols_factor, turned = halves(cols_factor), halves(inverse.T)
    tall = row_count // 4
    for at in range(0, row_count, tall):
        rows = slice(at, at + tall)
        factor = dot32(halves(gram_part(rows, slice(0, NB), t * row_count + at, 0)[0]), turned)
        value, row_ids = gram_part(rows, own, t * row_count + at, s * col_count)
        value = value - dot32(halves(factor), cols_factor)
        value = jnp.where(row_ids < NB, 0.0, value)
        out_ref[rows, NB:col_count] = value[:, NB:]
        out_ref[rows, 0:NB] = jnp.where(s == 0, factor, value[:, :NB])


def swap(x, axis, bit):
    return lax.ppermute(x, axis, [(i, i ^ bit) for i in range(lax.axis_size(axis))])


def shards(snapshots, pod_basis, inputs):
    modes = pod_basis.shape[1]
    space_count, time_count = lax.axis_size("space"), lax.axis_size("tm")
    t, s = lax.axis_index("tm"), lax.axis_index("space")
    local = snapshots.shape[1]
    snaps = local * time_count
    depth = local // space_count
    plan = make_plan(modes, inputs.shape[0], time_count, space_count)

    def some(x, bit, wanted):
        pairs = [
            (a * time_count + b, a * time_count + (b ^ bit))
            for a in range(space_count)
            for b in range(time_count)
            if a == space_count - 1 or b in wanted
        ]
        return lax.ppermute(x, ("space", "tm"), pairs)

    u_near = some(inputs, 1, (2,))
    u_far = some(inputs, 2, (0, 1))

    limit = 1200.0 * 0.0625 * snapshots.shape[0] * space_count
    shrink = 2.0 ** -max(0, math.ceil(math.log2(limit / 65000.0)))
    part = jnp.einsum("dr,ds->rs", pod_basis, snapshots, preferred_element_type=jnp.float32)
    part = (part * shrink).astype(jnp.float16)
    part = part.reshape(modes, space_count, depth).transpose(1, 0, 2)
    part = lax.all_to_all(part, "space", 0, 0, tiled=False)
    mine = jnp.sum(part.astype(jnp.float32), axis=0).astype(jnp.float16)[None]

    def partners(axes):
        return [a ^ b for a in (0, axes[0]) for b in (0, axes[-1])][1:] if len(axes) > 1 else axes

    def crossing(a_bit, b_bit):
        return [
            (a * time_count + b, (a ^ a_bit) * time_count + (b ^ b_bit))
            for a in range(space_count)
            for b in range(time_count)
        ]

    bits = [1 << b for b in reversed(range(1, space_count.bit_length() - 1))]
    levels = [bits[at : at + 2] for at in range(0, len(bits), 2)]
    order = [0]
    for level in levels:
        order = order + [o ^ bit for bit in partners(level) for o in order]
    order = jnp.asarray(order + [o ^ 1 for o in order], jnp.int32)
    where = jnp.concatenate([jnp.stack([t, s]), s ^ order]).astype(jnp.int32)
    mine, u_near, where = lax.optimization_barrier((mine, u_near, where))
    for level in levels:
        mine = jnp.concatenate([mine] + [swap(mine, "space", bit) for bit in partners(level)], axis=0)
    mine, u_far = lax.optimization_barrier((mine, u_far))
    wide = mine.astype(jnp.float32)
    energy = jnp.sum(wide * wide, axis=(0, 2))[None]
    moves = [(0, 2), (1, 0), (1, 2)]
    energy = energy + swap(energy, "tm", 1)
    energy = [energy] + [lax.ppermute(energy, ("space", "tm"), crossing(*move)) for move in moves]
    mine, energy = lax.optimization_barrier((mine, energy))

    def both(x):
        return x.astype(jnp.float32), swap(x, "tm", 1).astype(jnp.float32)

    beside = swap(mine, "space", 1)
    far = swap(mine, "tm", 2)
    cross = lax.ppermute(mine, ("space", "tm"), crossing(1, 2))
    us = [inputs, u_near]
    acc = gram_call(plan, snaps, shrink, where, [[x] for x in both(mine)], us, [0, 1], [0, 0], energy)
    acc, beside, far, cross, u_far = lax.optimization_barrier((acc, beside, far, cross, u_far))
    us = us + [u_far, some(u_far, 1, (2,))]
    xs = [[x] for x in both(beside) + both(far) + both(cross)]
    return gram_call(plan, snaps, shrink, where, xs, us, [0, 1, 2, 3, 2, 3], [1, 1, 0, 0, 1, 1], energy, acc)


def solution(mesh):
    return jax.shard_map(
        shards,
        mesh=mesh,
        in_specs=(P("space", "tm"), P("space", None), P(None, "tm")),
        out_specs=P("tm", "space"),
        check_vma=False,
    )
```
